32 devices in a mesh: mic: 8 (over y, x, core), proj: 4 (over z).
Axes of the slice: x: 2, y: 2, z: 4, core: 2. Of those that a mesh axis runs over, the one named last changes fastest.
Arguments:
- map_slabs: bfloat16 [20, 8, 256, 256], P('proj'), may hold values from -1.25 to 1.25
- slot_slab: int32 [20], P('proj'), may hold values from -1 to 11, as said below
- orient_index: int32 [4], replicated, may hold values from 0 to 255
- slab_lo: int32 [4], replicated, may hold values from 0 to 4
- slab_hi: int32 [4], replicated, may hold values from 8 to 12
- tile_spectrum: bfloat16 [32, 512, 1024], P(('mic', 'proj')), may hold values from -6 to 6
- prev_max: float32 [32, 512, 512], P(('mic', 'proj')), may hold values from -6 to 6
- prev_sum: float32 [32, 512, 512], P(('mic', 'proj')), may hold values from -12 to 12
- prev_sumsq: float32 [32, 512, 512], P(('mic', 'proj')), may hold values from 0.5 to 4
Outputs:
- best_score: float32 [32, 512, 512], P(('mic', 'proj'))
- score_sum: float32 [32, 512, 512], P(('mic', 'proj'))
- score_sumsq: float32 [32, 512, 512], P(('mic', 'proj'))
The draws below stay inside these ranges and needn't reach their ends.
Inputs may be any that keep to these rules, and one draw needn't show every extreme that they name: `slot_slab`: each slab 0 to 11 stands in exactly one slot; every other slot holds -1. One index of proj holds 5 slabs; the others may hold fewer, and may hold none.
All inputs are finite; a program needn't handle non-finite values.
Results may differ from the reference program's by a relative error of at most 0.0057.
Values may be sent and summed in bfloat16 or wider, within the bound.
No kernel may reach another device: no remote copies, remote signals or barrier semaphores. Data moves between devices by JAX's collectives and lax.ppermute only.
A program may use at most 128 MiB of HBM per device.

```python
import math
import jax
import jax.numpy as jnp
from jax import lax

BOX = 256
TILE = 512
SLAB_Z = 8
SLABS = 12
SLOTS_DEV = 5
ORI = 4
NORI = 256
SLOTS = 20
TILES = 32


def draw_slot_slab(key, part):
    key_heavy = jax.random.fold_in(key, 11)
    key_order = jax.random.fold_in(key, 12)
    key_slabs = jax.random.fold_in(key, 13)
    owner_count = SLOTS // SLOTS_DEV
    heavy = jax.random.randint(key_heavy, (), 0, owner_count)
    owners = jnp.arange(SLOTS, dtype=jnp.int32) // SLOTS_DEV
    shuffled = jax.random.permutation(key_order, SLOTS).astype(jnp.int32)
    ranking = jnp.where(owners == heavy, -1 - jnp.arange(SLOTS, dtype=jnp.int32), shuffled)
    ordering = jnp.argsort(ranking, stable=True)
    chosen = ordering[:SLABS]
    slab_ids = jax.random.permutation(key_slabs, SLABS).astype(jnp.int32)
    return jnp.full((SLOTS,), -1, jnp.int32).at[chosen].set(slab_ids)


def place_ends(array, rng, least, high):
    place = [jax.random.randint(jax.random.fold_in(rng, axis), (), 0, length) for axis, length in enumerate(array.shape)]
    main_axis = array.shape.index(max(array.shape))
    neighbour = place[:main_axis] + [(place[main_axis] + 1) % array.shape[main_axis]] + place[main_axis + 1:]
    return array.at[tuple(place)].set(least).at[tuple(neighbour)].set(high)


def level_of(key, dims, pieces, low, largest):
    def one(dim, parts):
        steps = jax.random.uniform(jax.random.fold_in(jax.random.fold_in(key, 6), dim), (parts,), jnp.float32, low / len(pieces), largest / len(pieces))
        return jnp.repeat(jnp.exp(steps), dims[dim] // parts).reshape((-1,) + (1,) * (len(dims) - dim - 1))

    factor_of = one(*pieces[0])
    for cut in pieces[1:]:
        factor_of = factor_of * one(*cut)
    return factor_of


def gaussian(rng, dims, spread, limit, shards=(), kind=jnp.bfloat16):
    array = jax.random.normal(rng, dims, jnp.float32) * spread
    if len(shards) > 0:
        array = level_of(rng, dims, shards, -0.22, 0.18) * array
    return jnp.clip(array, min=-limit, max=limit).astype(kind)


def setup_inputs(seed: int = 0) -> dict:
    splits = jax.random.split(jax.random.key(seed), 10)
    map_slabs = gaussian(splits[0], (SLOTS, SLAB_Z, BOX, BOX), (2 / (SLABS * SLAB_Z) ** 0.5), 1.25, ((0, 4),))
    slot_slab = draw_slot_slab(jax.random.fold_in(splits[9], 71), 0)
    orient_index = place_ends(jax.random.randint(splits[2], (ORI,), 0, NORI), jax.random.fold_in(splits[2], 1), 0, NORI - 1).astype(jnp.int32)
    slab_lo = place_ends(jax.random.randint(splits[3], (ORI,), 0, SLABS // 3 + 1), jax.random.fold_in(splits[3], 1), 0, (SLABS // 3 + 1) - 1).astype(jnp.int32)
    slab_hi = place_ends(jax.random.randint(splits[4], (ORI,), 2 * SLABS // 3, SLABS + 1), jax.random.fold_in(splits[4], 1), 2 * SLABS // 3, SLABS).astype(jnp.int32)
    tile_spectrum = gaussian(splits[5], (TILES, TILE, 2 * TILE), 1.0, 6.0, ((0, 32),))
    prev_max = gaussian(splits[6], (TILES, TILE, TILE), 1.0, 6.0, ((0, 32),), jnp.float32)
    prev_sum = gaussian(splits[7], (TILES, TILE, TILE), 2.0, 12.0, ((0, 32),), jnp.float32)
    prev_sumsq = jnp.clip(0.5 + 3.5 * jax.random.uniform(splits[8], (TILES, TILE, TILE), jnp.float32) ** level_of(splits[8], (TILES, TILE, TILE), ((0, 32),), -0.2, 0.2), 0.5, 4.0)
    return dict(map_slabs=map_slabs, slot_slab=slot_slab, orient_index=orient_index, slab_lo=slab_lo, slab_hi=slab_hi, tile_spectrum=tile_spectrum, prev_max=prev_max, prev_sum=prev_sum, prev_sumsq=prev_sumsq)


max_slope = 0.5
golden_angle = 2.399963

def rounded(value):
    return lax.optimization_barrier(value.astype(jnp.bfloat16)).astype(jnp.float32)

def matmul(left_op, right_op):
    return jnp.dot(left_op.astype(jnp.float32), right_op.astype(jnp.float32), precision=lax.Precision.HIGHEST)

def tent_weight(offsets):
    return jnp.maximum(0.0, 1.0 - jnp.abs(offsets))

def orient_slopes(orient_index):
    search_step = orient_index.astype(jnp.float32)
    radius = max_slope * jnp.sqrt((search_step + 0.5) / NORI)
    return (radius * jnp.cos(golden_angle * search_step), radius * jnp.sin(golden_angle * search_step))

def phase_parts(freq_count, pixel_count, length):
    freqs = jnp.arange(freq_count, dtype=jnp.int32)[:, None]
    pixels = jnp.arange(pixel_count, dtype=jnp.int32)[None, :]
    turn_frac = (freqs * pixels % length).astype(jnp.float32) / length
    norm_scale = 1.0 / math.sqrt(length)
    return (jnp.cos(2.0 * math.pi * turn_frac) * norm_scale, jnp.sin(2.0 * math.pi * turn_frac) * norm_scale)

def dft_tables(box_edge, tile_edge):
    row_cos, row_sin = phase_parts(box_edge, tile_edge, tile_edge)
    row_table = rounded(jnp.concatenate([row_cos, -row_sin], axis=1))
    col_cos, col_sin = phase_parts(tile_edge, box_edge, tile_edge)
    column_table = rounded(jnp.concatenate([col_cos, -col_sin], axis=0))
    full_cos, full_sin = phase_parts(tile_edge, tile_edge, tile_edge)
    inverse_table = rounded(jnp.concatenate([full_cos, full_sin], axis=1))
    final_table = rounded(jnp.concatenate([full_cos, -full_sin], axis=1))
    return (row_table, column_table, inverse_table, final_table)

def correlate(row_block, spectrum_tile, column_table, inverse_table, final_table):
    edge = spectrum_tile.shape[0]
    stacked = matmul(column_table, row_block)
    real_part = stacked[:edge, :edge] - stacked[edge:, edge:]
    imag_part = stacked[:edge, edge:] + stacked[edge:, :edge]
    micro_real = spectrum_tile[:, :edge].astype(jnp.float32)
    micro_imag = spectrum_tile[:, edge:].astype(jnp.float32)
    product = rounded(jnp.concatenate([micro_real * real_part + micro_imag * imag_part, micro_imag * real_part - micro_real * imag_part], axis=0))
    halfway = matmul(product, inverse_table)
    half_real = halfway[:edge, :edge] - halfway[edge:, edge:]
    half_imag = halfway[:edge, edge:] + halfway[edge:, :edge]
    half_stack = rounded(jnp.concatenate([half_real, half_imag], axis=0))
    return matmul(final_table, half_stack)

def reference(map_slabs, slot_slab, orient_index, slab_lo, slab_hi, tile_spectrum, prev_max, prev_sum, prev_sumsq):
    slope_x, slope_y = orient_slopes(orient_index)
    center = (SLABS * SLAB_Z - 1) / 2.0
    positions = jnp.arange(BOX, dtype=jnp.int32).astype(jnp.float32)
    within = jnp.arange(SLAB_Z, dtype=jnp.int32)
    projection = jnp.zeros((ORI, BOX, BOX), jnp.float32)
    for slot_number in range(SLOTS):
        slab_id = slot_slab[slot_number]
        depths = (slab_id * SLAB_Z + within).astype(jnp.float32) - center
        shift_x = slope_x[:, None] * depths[None, :]
        shift_y = slope_y[:, None] * depths[None, :]
        left_tent = rounded(tent_weight(positions[None, None, None, :] - positions[None, None, :, None] - shift_x[:, :, None, None]))
        right_tent = rounded(tent_weight(positions[None, None, None, :] - positions[None, None, :, None] - shift_y[:, :, None, None]))
        slab_map = map_slabs[slot_number].astype(jnp.float32)
        sheared = rounded(jnp.einsum('ojax,jxy->ojay', left_tent, slab_map, precision=lax.Precision.HIGHEST))
        slab_term = jnp.einsum('ojay,ojby->oab', sheared, right_tent, precision=lax.Precision.HIGHEST)
        inside = ((slab_id >= slab_lo) & (slab_id < slab_hi)).astype(jnp.float32)
        projection = projection + inside[:, None, None] * slab_term
    template = rounded(projection)
    row_table, column_table, inverse_table, final_table = dft_tables(BOX, TILE)
    row_spectrum = rounded(jnp.einsum('oay,yk->oak', template, row_table, precision=lax.Precision.HIGHEST))

    def per_tile(operands):
        spectrum_tile, best_seen, totals, squares = operands

        def per_orient(orient, running):
            best_run, total_run, square_run = running
            scores = correlate(row_spectrum[orient], spectrum_tile, column_table, inverse_table, final_table)
            return (jnp.maximum(best_run, scores), total_run + scores, square_run + scores * scores)
        return lax.fori_loop(0, ORI, per_orient, (best_seen, totals, squares))
    best_score, score_sum, score_sumsq = lax.map(per_tile, (tile_spectrum, prev_max, prev_sum, prev_sumsq))
    return (best_score, score_sum, score_sumsq)
```

```python
import math

import jax
import jax.numpy as jnp
import ml_dtypes
import numpy as np
from jax import lax
from jax.experimental import pallas as pl
from jax.experimental.pallas import tpu as pltpu
from jax.sharding import PartitionSpec as P

SLAB_Z = 8
SLABS = 12
NORI = 256
MAX_SLOPE = 0.5
GOLDEN_ANGLE = 2.399963

F32 = jnp.float32
BF16 = jnp.bfloat16


def phase_tables(edge):
    index = np.arange(edge, dtype=np.int64)
    turn = (index[:, None] * index[None, :] % edge).astype(np.float64) / edge
    scale = 1.0 / math.sqrt(edge)
    cos = (np.cos(2.0 * np.pi * turn) * scale).astype(np.float32)
    sin = (np.sin(2.0 * np.pi * turn) * scale).astype(np.float32)
    return cos.astype(ml_dtypes.bfloat16), sin.astype(ml_dtypes.bfloat16)


def class_order(edge):
    return np.concatenate([np.arange(r, edge, 4) for r in range(4)])


def constants(box, edge):
    cos, sin = phase_tables(edge)
    quarter = edge // 4
    order = class_order(edge)
    cg, sg = cos[order, :box].T, sin[order, :box].T
    row = np.block([[cg, -sg], [-sg, -cg]])
    quad = []
    for r in range(4):
        c, s = cos[r::4, :quarter], sin[r::4, :quarter]
        quad.append(np.block([[c, s], [-s, c]]))
    quad = np.stack(quad)
    quad_t = np.ascontiguousarray(quad.transpose(0, 2, 1))
    pick = np.zeros((2 * edge, edge), np.float32)
    pick[np.arange(edge), order] = 1.0
    pick[edge + np.arange(edge), (-order) % edge] = 1.0
    pick_rows = pick.astype(ml_dtypes.bfloat16)
    pick_cols = np.concatenate([0.5 * pick[:edge].T, 0.5 * pick[edge:].T], axis=0).astype(ml_dtypes.bfloat16)
    return tuple(jnp.asarray(x) for x in (row, quad, quad_t, pick_rows, pick_cols))


def dot(a, b):
    return jnp.dot(a, b, preferred_element_type=F32)


def tent(offsets):
    return jnp.maximum(0.0, 1.0 - jnp.abs(offsets))


def project_kernel(rows, window, slot_ref, orient_ref, lo_ref, hi_ref, map_ref, out_ref, slabs, diff_x, diff_y, acc, sems):
    slots, depth, box = map_ref.shape[0], map_ref.shape[1], map_ref.shape[2]
    me = lax.axis_index("mic")
    orient = (me % 2) * 2 + (me // 2) % 2
    first = (me // 4) * rows
    base = jnp.clip(first - 32, 0, box - window)
    base = pl.multiple_of(base // 16 * 16, 16)

    def fetch(i):
        return pltpu.make_async_copy(map_ref.at[i, :, pl.ds(base, window), :], slabs.at[i], sems.at[i])

    for i in range(slots):
        fetch(i).start()

    step = jnp.full((8, 128), orient_ref[orient], jnp.int32).astype(F32)
    radius = MAX_SLOPE * jnp.sqrt((step + 0.5) / NORI)
    slope_x = jnp.max(radius * jnp.cos(GOLDEN_ANGLE * step))
    slope_y = jnp.max(radius * jnp.sin(GOLDEN_ANGLE * step))
    low, high = lo_ref[orient], hi_ref[orient]

    a = lax.broadcasted_iota(jnp.int32, (rows, window), 0)
    b = lax.broadcasted_iota(jnp.int32, (rows, window), 1)
    diff_x[...] = (b - a + (base - first)).astype(F32)
    d = lax.broadcasted_iota(jnp.int32, (box, box), 0)
    c = lax.broadcasted_iota(jnp.int32, (box, box), 1)
    diff_y[...] = (d - c).astype(F32)
    acc[...] = jnp.zeros_like(acc)

    for i in range(slots):
        fetch(i).wait()
        slab = slot_ref[i]

        @pl.when((slab >= low) & (slab < high))
        def _():
            total = None
            for j in range(depth):
                z = (slab * depth + j).astype(F32) - (SLABS * SLAB_Z - 1) / 2.0
                left = tent(diff_x[...] - slope_x * z).astype(BF16)
                sheared = dot(left, slabs[i, j]).astype(BF16)
                right = tent(diff_y[...] - slope_y * z).astype(BF16)
                term = dot(sheared, right)
                total = term if total is None else total + term
            acc[...] += total

    out_ref[...] = acc[...].astype(BF16)


def project(map_slabs, slot_slab, orient_index, slab_lo, slab_hi, rows):
    slots, depth, box = map_slabs.shape[:3]
    blocks = box // rows
    window = min(box, rows + 32 * min(2, blocks - 1))
    smem = pl.BlockSpec(memory_space=pltpu.SMEM)
    return pl.pallas_call(
        lambda *refs: project_kernel(rows, window, *refs),
        out_shape=jax.ShapeDtypeStruct((rows, box), BF16),
        in_specs=[smem, smem, smem, smem, pl.BlockSpec(memory_space=pltpu.HBM)],
        out_specs=pl.BlockSpec(memory_space=pltpu.VMEM),
        scratch_shapes=[
            pltpu.VMEM((slots, depth, window, box), BF16),
            pltpu.VMEM((rows, window), F32),
            pltpu.VMEM((box, box), F32),
            pltpu.VMEM((rows, box), F32),
            pltpu.SemaphoreType.DMA((slots,)),
        ],
        compiler_params=pltpu.CompilerParams(vmem_limit_bytes=32 << 20),
        name="project",
    )(slot_slab, orient_index, slab_lo, slab_hi, map_slabs)


def hermitian_kernel(tile_ref, rows_ref, cols_ref, real_ref, imag_ref, picked):
    edge = real_ref.shape[0]
    picked[...] = dot(rows_ref[...], tile_ref[...]).astype(BF16)
    real = jnp.concatenate([picked[:edge, :edge], picked[edge:, :edge]], axis=1)
    real_ref[...] = dot(real, cols_ref[...])
    imag = jnp.concatenate([picked[:edge, edge:], -picked[edge:, edge:]], axis=1)
    imag_ref[...] = dot(imag, cols_ref[...])


def hermitian(tile, pick_rows, pick_cols):
    edge = tile.shape[0]
    vmem = pl.BlockSpec(memory_space=pltpu.VMEM)
    return pl.pallas_call(
        hermitian_kernel,
        out_shape=[jax.ShapeDtypeStruct((edge, edge), F32)] * 2,
        in_specs=[vmem] * 3,
        out_specs=[vmem] * 2,
        scratch_shapes=[pltpu.VMEM((2 * edge, 2 * edge), BF16)],
        compiler_params=pltpu.CompilerParams(vmem_limit_bytes=32 << 20),
        cost_estimate=pl.CostEstimate(flops=8 * edge**3 * 2, bytes_accessed=12 * edge * edge, transcendentals=0),
        name="hermitian",
    )(tile, pick_rows, pick_cols)


def half_transform(pieces_ref, real_ref, imag_ref, row_ref, quad_ref, quadt_ref, stack, half):
    count, rows, box = pieces_ref.shape
    edge = real_ref.shape[0]
    quarter = edge // 4
    for q in range(count):
        stack[(q // 2) * rows : (q // 2 + 1) * rows, (q % 2) * box : (q % 2 + 1) * box] = pieces_ref[q]
    width = 2 * quarter
    for gh in range(edge // width):
        cols = slice(gh * width, (gh + 1) * width)
        rr = dot(stack[...], row_ref[:, gh * width : (gh + 1) * width])
        ri = dot(stack[...], row_ref[:, edge + gh * width : edge + (gh + 1) * width])
        r0, r1 = rr[:quarter], rr[quarter:]
        i0, i1 = ri[:quarter], ri[quarter:]
        inputs = ((r0 + r1, i0 + i1), (r0 + i1, i0 - r1), (r0 - r1, i0 - i1), (r0 - i1, i0 + r1))
        parts = []
        for r in range(4):
            u = jnp.concatenate(inputs[r], axis=0).astype(BF16)
            spec = dot(quad_ref[r], u)
            sr, si = spec[:quarter], spec[quarter:]
            fr = slice(r * quarter, (r + 1) * quarter)
            tr, ti = real_ref[fr, cols], imag_ref[fr, cols]
            product = jnp.concatenate([tr * sr + ti * si, ti * sr - tr * si], axis=0).astype(BF16)
            parts.append(dot(quadt_ref[r], product))
        ar, ai = parts[0][:quarter] + parts[2][:quarter], parts[0][quarter:] + parts[2][quarter:]
        br, bi = parts[0][:quarter] - parts[2][:quarter], parts[0][quarter:] - parts[2][quarter:]
        cr, ci = parts[1][:quarter] + parts[3][:quarter], parts[1][quarter:] + parts[3][quarter:]
        dr, di = parts[1][:quarter] - parts[3][:quarter], parts[1][quarter:] - parts[3][quarter:]
        outs = ((ar + cr, ai + ci), (br - di, bi + dr), (ar - cr, ai - ci), (br + di, bi - dr))
        for k in range(4):
            xs = slice(k * quarter, (k + 1) * quarter)
            hr, hi = outs[k][0].astype(BF16), outs[k][1].astype(BF16)
            for t in range(2):
                lanes = slice(t * quarter, (t + 1) * quarter)
                start = (2 * gh + t) * width
                half[xs, start : start + quarter] = hr[:, lanes]
                half[xs, start + quarter : start + width] = hi[:, lanes]


def first_kernel(pieces_ref, real_ref, imag_ref, row_ref, quad_ref, quadt_ref, half_ref, stack):
    half_transform(pieces_ref, real_ref, imag_ref, row_ref, quad_ref, quadt_ref, stack, half_ref)


def first_pair(pieces, th_real, th_imag, row, quad, quad_t):
    box, edge = pieces.shape[2], th_real.shape[0]
    vmem = pl.BlockSpec(memory_space=pltpu.VMEM)
    return pl.pallas_call(
        first_kernel,
        out_shape=jax.ShapeDtypeStruct((edge, 2 * edge), BF16),
        in_specs=[vmem] * 6,
        out_specs=vmem,
        scratch_shapes=[pltpu.VMEM((box, 2 * box), BF16)],
        compiler_params=pltpu.CompilerParams(vmem_limit_bytes=40 << 20),
        cost_estimate=pl.CostEstimate(flops=6 * edge**3, bytes_accessed=12 * edge * edge, transcendentals=0),
        name="first_pair",
    )(pieces, th_real, th_imag, row, quad, quad_t)


def scores_of(half, quad_ref, quarter):
    width = 2 * quarter
    f = [dot(half[:, s * width : (s + 1) * width], quad_ref[s]) for s in range(4)]
    re = [x[:, :quarter] for x in f]
    im = [x[:, quarter:] for x in f]
    ar, ai, br, bi = re[0] + re[2], im[0] + im[2], re[0] - re[2], im[0] - im[2]
    cr, ci, dr, di = re[1] + re[3], im[1] + im[3], re[1] - re[3], im[1] - im[3]
    return ((ar + cr, ai + ci), (br - di, bi + dr), (ar - cr, ai - ci), (br + di, bi - dr))


def second_kernel(
    pieces_ref, half_ref, real_ref, imag_ref, row_ref, quad_ref, quadt_ref, max_ref, sum_ref, sq_ref,
    best_ref, total_ref, square_ref, stack, other,
):
    block = max_ref.shape[1]
    quarter = max_ref.shape[2] // 4
    step = pl.program_id(0)

    @pl.when(step == 0)
    def _():
        half_transform(pieces_ref, real_ref, imag_ref, row_ref, quad_ref, quadt_ref, stack, other)

    xs = pl.ds(pl.multiple_of(step * block, block), block)
    one = scores_of(half_ref[xs, :], quad_ref, quarter)
    two = scores_of(other[xs, :], quad_ref, quarter)
    for k in range(4):
        ys = slice(k * quarter, (k + 1) * quarter)
        best, total, square = max_ref[0, :, ys], sum_ref[0, :, ys], sq_ref[0, :, ys]
        for score in (*one[k], *two[k]):
            best = jnp.maximum(best, score)
            total = total + score
            square = square + score * score
        best_ref[0, :, ys] = best
        total_ref[0, :, ys] = total
        square_ref[0, :, ys] = square


def second_pair(pieces, half, th_real, th_imag, row, quad, quad_t, prev_max, prev_sum, prev_sumsq):
    box, edge = pieces.shape[2], th_real.shape[0]
    block = edge // 4

    def whole(x):
        return pl.BlockSpec(x.shape, lambda i, n=x.ndim: (0,) * n)

    stat = pl.BlockSpec((1, block, edge), lambda i: (0, i, 0))
    return pl.pallas_call(
        second_kernel,
        grid=(edge // block,),
        out_shape=[jax.ShapeDtypeStruct(prev_max.shape, F32)] * 3,
        in_specs=[whole(x) for x in (pieces, half, th_real, th_imag, row, quad, quad_t)] + [stat] * 3,
        out_specs=[stat] * 3,
        scratch_shapes=[pltpu.VMEM((box, 2 * box), BF16), pltpu.VMEM((edge, 2 * edge), BF16)],
        compiler_params=pltpu.CompilerParams(vmem_limit_bytes=48 << 20),
        cost_estimate=pl.CostEstimate(flops=10 * edge**3, bytes_accessed=40 * edge * edge, transcendentals=0),
        name="second_pair",
    )(pieces, half, th_real, th_imag, row, quad, quad_t, prev_max, prev_sum, prev_sumsq)


def swap(value, axis, offset):
    return lax.ppermute(value, axis, [(i, i ^ offset) for i in range(lax.axis_size(axis))])


def gather_group(value, low_bit, bits):
    mine = (lax.axis_index("mic") >> low_bit) & ((1 << bits) - 1)
    got = [(k, swap(value, "mic", k << low_bit)) for k in range(1, 1 << bits)]
    out = jnp.zeros((1 << bits,) + value.shape, value.dtype)
    for k, block in [(0, value)] + got:
        out = lax.dynamic_update_index_in_dim(out, block, mine ^ k, 0)
    return out.reshape((-1,) + value.shape[1:])


def body(map_slabs, slot_slab, orient_index, slab_lo, slab_hi, tile_spectrum, prev_max, prev_sum, prev_sumsq):
    box, edge = map_slabs.shape[2], tile_spectrum.shape[1]
    devices = lax.axis_size("mic")
    bits = devices.bit_length() - 1
    rows = box * 4 // devices
    row, quad, quad_t, pick_rows, pick_cols = constants(box, edge)

    part = project(map_slabs, slot_slab, orient_index, slab_lo, slab_hi, rows)
    got = [swap(part, "proj", k) for k in range(1, lax.axis_size("proj"))]
    th_real, th_imag = hermitian(tile_spectrum[0], pick_rows, pick_cols)
    total = part.astype(F32)
    for block in got:
        total = total + block.astype(F32)
    pieces = total.astype(BF16)[None]
    for low in range(1, bits, 2):
        pieces = gather_group(pieces, low, min(2, bits - low))
    others = swap(pieces, "mic", 1)
    half = first_pair(pieces, th_real, th_imag, row, quad, quad_t)
    return tuple(second_pair(others, half, th_real, th_imag, row, quad, quad_t, prev_max, prev_sum, prev_sumsq))


def solution(mesh):
    tiles = P(("mic", "proj"), None, None)
    in_specs = (P("proj", None, None, None), P("proj"), P(), P(), P(), tiles, tiles, tiles, tiles)
    return jax.shard_map(body, mesh=mesh, in_specs=in_specs, out_specs=(tiles,) * 3, check_vma=False)
```

```python
import math

import jax
import jax.numpy as jnp
import ml_dtypes
import numpy as np
from jax import lax
from jax.experimental import pallas as pl
from jax.experimental.pallas import tpu as pltpu
from jax.sharding import PartitionSpec as P

SLAB_Z = 8
SLABS = 12
NORI = 256
MAX_SLOPE = 0.5
GOLDEN_ANGLE = 2.399963

F32 = jnp.float32
BF16 = jnp.bfloat16
TAP = jnp.int16


def phase_tables(edge):
    index = np.arange(edge, dtype=np.int64)
    turn = (index[:, None] * index[None, :] % edge).astype(np.float64) / edge
    scale = 1.0 / math.sqrt(edge)
    cos = (np.cos(2.0 * np.pi * turn) * scale).astype(np.float32)
    sin = (np.sin(2.0 * np.pi * turn) * scale).astype(np.float32)
    return cos.astype(ml_dtypes.bfloat16), sin.astype(ml_dtypes.bfloat16)


def class_order(edge):
    return np.concatenate([np.arange(r, edge, 4) for r in range(4)])


def constants(box, edge):
    cos, sin = phase_tables(edge)
    quarter = edge // 4
    order = class_order(edge)
    cg, sg = cos[order, :box].T, sin[order, :box].T
    row = np.block([[cg, -sg], [-sg, -cg]])
    quad = []
    for r in range(4):
        c, s = cos[r::4, :quarter], sin[r::4, :quarter]
        quad.append(np.block([[c, s], [-s, c]]))
    quad = np.stack(quad)
    quad_t = np.ascontiguousarray(quad.transpose(0, 2, 1))
    return tuple(jnp.asarray(x) for x in (row, quad, quad_t))


def dot(a, b):
    return jnp.dot(a, b, preferred_element_type=F32)


def tent(offsets):
    return jnp.maximum(0.0, 1.0 - jnp.abs(offsets))


def two_taps(index, shift):
    whole = jnp.floor(shift)
    frac = shift - whole
    tap = whole.astype(jnp.int32)
    tap, next_tap = tap.astype(index.dtype), (tap + 1).astype(index.dtype)
    low = jnp.full(index.shape, 1.0 - frac, F32).astype(BF16)
    high = jnp.full(index.shape, frac, F32).astype(BF16)
    zero = jnp.zeros(index.shape, BF16)
    return jnp.where(index == tap, low, jnp.where(index == next_tap, high, zero))


def project_kernel(
    rows, window, slot_hbm, orient_hbm, lo_hbm, hi_hbm, map_ref, out_ref,
    slabs, diff_x, diff_y, sheared, right, acc, sems, slot_ref, orient_ref, lo_ref, hi_ref, param_sems,
):
    slots, depth, box = map_ref.shape[0], map_ref.shape[1], map_ref.shape[2]
    me = lax.axis_index("mic")
    orient = (me % 2) * 2 + (me // 2) % 2
    first = (me // 4) * rows
    base = jnp.clip(first - 32, 0, box - window)
    base = pl.multiple_of(base // 16 * 16, 16)

    def fetch(i):
        return pltpu.make_async_copy(map_ref.at[i, :, pl.ds(base, window), :], slabs.at[i], sems.at[i])

    params = [
        pltpu.make_async_copy(src, dst, param_sems.at[n])
        for n, (src, dst) in enumerate(((slot_hbm, slot_ref), (orient_hbm, orient_ref), (lo_hbm, lo_ref), (hi_hbm, hi_ref)))
    ]
    for copy in params:
        copy.start()
    for i in range(slots):
        fetch(i).start()

    for copy in params:
        copy.wait()
    step = jnp.full((8, 128), orient_ref[orient], jnp.int32).astype(F32)
    radius = MAX_SLOPE * jnp.sqrt((step + 0.5) / NORI)
    slope_x = jnp.max(radius * jnp.cos(GOLDEN_ANGLE * step))
    slope_y = jnp.max(radius * jnp.sin(GOLDEN_ANGLE * step))
    low, high = lo_ref[orient], hi_ref[orient]

    a = lax.broadcasted_iota(jnp.int32, (rows, window), 0)
    b = lax.broadcasted_iota(jnp.int32, (rows, window), 1)
    diff_x[...] = (b - a + (base - first)).astype(diff_x.dtype)
    d = lax.broadcasted_iota(jnp.int32, (box, box), 0)
    c = lax.broadcasted_iota(jnp.int32, (box, box), 1)
    diff_y[...] = (d - c).astype(diff_y.dtype)
    acc[...] = jnp.zeros_like(acc)
    right[...] = jnp.zeros_like(right)
    half = box // 2
    bands = ((slice(0, half + 32), slice(0, half)), (slice(half - 32, box), slice(half, box)))

    for i in range(slots):
        fetch(i).wait()
        slab = slot_ref[i]

        @pl.when((slab >= low) & (slab < high))
        def _():
            for j in range(depth):
                z = (slab * depth + j).astype(F32) - (SLABS * SLAB_Z - 1) / 2.0
                left = two_taps(diff_x[...], slope_x * z)
                sheared[:, j * box : (j + 1) * box] = dot(left, slabs[i, j]).astype(BF16)
                for ds, cs in bands:
                    right[j * box + ds.start : j * box + ds.stop, cs] = two_taps(diff_y[ds, cs], slope_y * z)
            acc[...] += dot(sheared[...], right[...])

    out_ref[...] = acc[...].astype(BF16)


def project(map_slabs, slot_slab, orient_index, slab_lo, slab_hi, rows):
    slots, depth, box = map_slabs.shape[:3]
    blocks = box // rows
    window = min(box, rows + 32 * min(2, blocks - 1))
    args = [pltpu.with_memory_space_constraint(x, pltpu.HBM) for x in (slot_slab, orient_index, slab_lo, slab_hi, map_slabs)]
    return pl.pallas_call(
        lambda *refs: project_kernel(rows, window, *refs),
        out_shape=jax.ShapeDtypeStruct((rows, box), BF16),
        in_specs=[pl.BlockSpec(memory_space=pltpu.HBM)] * 5,
        out_specs=pl.BlockSpec(memory_space=pltpu.VMEM),
        scratch_shapes=[
            pltpu.VMEM((slots, depth, window, box), BF16),
            pltpu.VMEM((rows, window), TAP),
            pltpu.VMEM((box, box), TAP),
            pltpu.VMEM((rows, depth * box), BF16),
            pltpu.VMEM((depth * box, box), BF16),
            pltpu.VMEM((rows, box), F32),
            pltpu.SemaphoreType.DMA((slots,)),
            pltpu.SMEM(slot_slab.shape, jnp.int32),
            pltpu.SMEM(orient_index.shape, jnp.int32),
            pltpu.SMEM(orient_index.shape, jnp.int32),
            pltpu.SMEM(orient_index.shape, jnp.int32),
            pltpu.SemaphoreType.DMA((4,)),
        ],
        compiler_params=pltpu.CompilerParams(vmem_limit_bytes=16 << 20),
        name="project",
    )(*args)


def total_kernel(*refs):
    total = refs[0][...].astype(F32)
    for ref in refs[1:-1]:
        total = total + ref[...].astype(F32)
    refs[-1][...] = total.astype(BF16)


def total_of(parts):
    vmem = pl.BlockSpec(memory_space=pltpu.VMEM)
    return pl.pallas_call(
        total_kernel,
        out_shape=jax.ShapeDtypeStruct(parts[0].shape, BF16),
        in_specs=[vmem] * len(parts),
        out_specs=vmem,
        compiler_params=pltpu.CompilerParams(vmem_limit_bytes=2 << 20),
        name="total",
    )(*parts)


def hermitian_kernel(tile_ref, real_ref, imag_ref, picked):
    edge = real_ref.shape[0]
    quarter = edge // 4

    def pick(dim):
        shape = (2 * edge, edge) if dim == 0 else (edge, 2 * edge)
        place = lax.broadcasted_iota(jnp.int32, shape, dim)
        freq = lax.broadcasted_iota(jnp.int32, shape, 1 - dim)
        inner = place & (edge - 1)
        wanted = 4 * (inner & (quarter - 1)) + inner // quarter
        wanted = jnp.where(place < edge, wanted, (edge - wanted) & (edge - 1))
        return freq == wanted

    rows = jnp.where(pick(0), 1.0, 0.0).astype(BF16)
    picked[...] = dot(rows, tile_ref[...]).astype(BF16)
    cols = jnp.where(pick(1), 0.5, 0.0).astype(BF16)
    cols = jnp.concatenate([cols[:, :edge], cols[:, edge:]], axis=0)
    real = jnp.concatenate([picked[:edge, :edge], picked[edge:, :edge]], axis=1)
    real_ref[...] = dot(real, cols)
    imag = jnp.concatenate([picked[:edge, edge:], -picked[edge:, edge:]], axis=1)
    imag_ref[...] = dot(imag, cols)


def hermitian(tile):
    edge = tile.shape[0]
    vmem = pl.BlockSpec(memory_space=pltpu.VMEM)
    return pl.pallas_call(
        hermitian_kernel,
        out_shape=[jax.ShapeDtypeStruct((edge, edge), F32)] * 2,
        in_specs=[vmem],
        out_specs=[vmem] * 2,
        scratch_shapes=[pltpu.VMEM((2 * edge, 2 * edge), BF16)],
        compiler_params=pltpu.CompilerParams(vmem_limit_bytes=16 << 20),
        cost_estimate=pl.CostEstimate(flops=8 * edge**3 * 2, bytes_accessed=12 * edge * edge, transcendentals=0),
        name="hermitian",
    )(tile)


def half_transform(pieces_ref, real_ref, imag_ref, row_ref, quad_ref, quadt_ref, stack, half):
    count, rows, box = pieces_ref.shape
    edge = real_ref.shape[0]
    quarter = edge // 4
    for q in range(count):
        stack[(q // 2) * rows : (q // 2 + 1) * rows, (q % 2) * box : (q % 2 + 1) * box] = pieces_ref[q]
    width = 2 * quarter
    for gh in range(edge // width):
        cols = slice(gh * width, (gh + 1) * width)
        rr = dot(stack[...], row_ref[:, gh * width : (gh + 1) * width])
        ri = dot(stack[...], row_ref[:, edge + gh * width : edge + (gh + 1) * width])
        r0, r1 = rr[:quarter], rr[quarter:]
        i0, i1 = ri[:quarter], ri[quarter:]
        inputs = ((r0 + r1, i0 + i1), (r0 + i1, i0 - r1), (r0 - r1, i0 - i1), (r0 - i1, i0 + r1))
        parts = []
        for r in range(4):
            u = jnp.concatenate(inputs[r], axis=0).astype(BF16)
            spec = dot(quad_ref[r], u)
            sr, si = spec[:quarter], spec[quarter:]
            fr = slice(r * quarter, (r + 1) * quarter)
            tr, ti = real_ref[fr, cols], imag_ref[fr, cols]
            product = jnp.concatenate([tr * sr + ti * si, ti * sr - tr * si], axis=0).astype(BF16)
            parts.append(dot(quadt_ref[r], product))
        ar, ai = parts[0][:quarter] + parts[2][:quarter], parts[0][quarter:] + parts[2][quarter:]
        br, bi = parts[0][:quarter] - parts[2][:quarter], parts[0][quarter:] - parts[2][quarter:]
        cr, ci = parts[1][:quarter] + parts[3][:quarter], parts[1][quarter:] + parts[3][quarter:]
        dr, di = parts[1][:quarter] - parts[3][:quarter], parts[1][quarter:] - parts[3][quarter:]
        outs = ((ar + cr, ai + ci), (br - di, bi + dr), (ar - cr, ai - ci), (br + di, bi - dr))
        for k in range(4):
            xs = slice(k * quarter, (k + 1) * quarter)
            hr, hi = outs[k][0].astype(BF16), outs[k][1].astype(BF16)
            for t in range(2):
                lanes = slice(t * quarter, (t + 1) * quarter)
                start = (2 * gh + t) * width
                half[xs, start : start + quarter] = hr[:, lanes]
                half[xs, start + quarter : start + width] = hi[:, lanes]


def first_kernel(pieces_ref, real_ref, imag_ref, row_ref, quad_ref, quadt_ref, half_ref, stack):
    half_transform(pieces_ref, real_ref, imag_ref, row_ref, quad_ref, quadt_ref, stack, half_ref)


def first_pair(pieces, th_real, th_imag, row, quad, quad_t):
    box, edge = pieces.shape[2], th_real.shape[0]
    vmem = pl.BlockSpec(memory_space=pltpu.VMEM)
    return pl.pallas_call(
        first_kernel,
        out_shape=jax.ShapeDtypeStruct((edge, 2 * edge), BF16),
        in_specs=[vmem] * 6,
        out_specs=vmem,
        scratch_shapes=[pltpu.VMEM((box, 2 * box), BF16)],
        compiler_params=pltpu.CompilerParams(vmem_limit_bytes=12 << 20),
        cost_estimate=pl.CostEstimate(flops=6 * edge**3, bytes_accessed=12 * edge * edge, transcendentals=0),
        name="first_pair",
    )(pieces, th_real, th_imag, row, quad, quad_t)


def scores_of(half, quad_ref, quarter):
    width = 2 * quarter
    f = [dot(half[:, s * width : (s + 1) * width], quad_ref[s]) for s in range(4)]
    re = [x[:, :quarter] for x in f]
    im = [x[:, quarter:] for x in f]
    ar, ai, br, bi = re[0] + re[2], im[0] + im[2], re[0] - re[2], im[0] - im[2]
    cr, ci, dr, di = re[1] + re[3], im[1] + im[3], re[1] - re[3], im[1] - im[3]
    return ((ar + cr, ai + ci), (br - di, bi + dr), (ar - cr, ai - ci), (br + di, bi - dr))


def second_kernel(
    block, pieces_ref, half_ref, real_ref, imag_ref, row_ref, quad_ref, quadt_ref, max_ref, sum_ref, sq_ref,
    best_ref, total_ref, square_ref, stack, other, best_out, total_out, square_out, sems,
):
    edge = max_ref.shape[2]
    quarter = edge // 4
    half_transform(pieces_ref, real_ref, imag_ref, row_ref, quad_ref, quadt_ref, stack, other)
    copies = []
    for step in range(edge // block):
        xs = slice(step * block, (step + 1) * block)
        one = scores_of(half_ref[xs, :], quad_ref, quarter)
        two = scores_of(other[xs, :], quad_ref, quarter)
        for k in range(4):
            ys = slice(k * quarter, (k + 1) * quarter)
            best, total, square = max_ref[0, xs, ys], sum_ref[0, xs, ys], sq_ref[0, xs, ys]
            for score in (*one[k], *two[k]):
                best = jnp.maximum(best, score)
                total = total + score
                square = square + score * score
            best_out[xs, ys] = best
            total_out[xs, ys] = total
            square_out[xs, ys] = square
        for n, (src, dst) in enumerate(((best_out, best_ref), (total_out, total_ref), (square_out, square_ref))):
            copy = pltpu.make_async_copy(src.at[xs, :], dst.at[0, xs, :], sems.at[step, n])
            copy.start()
            copies.append(copy)
    for copy in copies:
        copy.wait()


def second_pair(pieces, half, th_real, th_imag, row, quad, quad_t, prev_max, prev_sum, prev_sumsq):
    box, edge = pieces.shape[2], th_real.shape[0]
    block = edge // 4
    vmem = pl.BlockSpec(memory_space=pltpu.VMEM)
    return pl.pallas_call(
        lambda *refs: second_kernel(block, *refs),
        out_shape=[jax.ShapeDtypeStruct(prev_max.shape, F32)] * 3,
        in_specs=[vmem] * 10,
        out_specs=[pl.BlockSpec(memory_space=pltpu.HBM)] * 3,
        scratch_shapes=[
            pltpu.VMEM((box, 2 * box), BF16),
            pltpu.VMEM((edge, 2 * edge), BF16),
            pltpu.VMEM((edge, edge), F32),
            pltpu.VMEM((edge, edge), F32),
            pltpu.VMEM((edge, edge), F32),
            pltpu.SemaphoreType.DMA((edge // block, 3)),
        ],
        compiler_params=pltpu.CompilerParams(vmem_limit_bytes=16 << 20),
        cost_estimate=pl.CostEstimate(flops=10 * edge**3, bytes_accessed=40 * edge * edge, transcendentals=0),
        name="second_pair",
    )(pieces, half, th_real, th_imag, row, quad, quad_t, prev_max, prev_sum, prev_sumsq)


def swap(value, axis, offset):
    return lax.ppermute(value, axis, [(i, i ^ offset) for i in range(lax.axis_size(axis))])


def assemble_kernel(low_bit, bits, *refs):
    mine = (lax.axis_index("mic") >> low_bit) & ((1 << bits) - 1)
    for k, ref in enumerate(refs[:-1]):
        refs[-1][mine ^ k] = ref[...]


def gather_group(value, low_bit, bits):
    got = [swap(value, "mic", k << low_bit) for k in range(1, 1 << bits)]
    vmem = pl.BlockSpec(memory_space=pltpu.VMEM)
    out = pl.pallas_call(
        lambda *refs: assemble_kernel(low_bit, bits, *refs),
        out_shape=jax.ShapeDtypeStruct((1 << bits,) + value.shape, value.dtype),
        in_specs=[vmem] * (1 << bits),
        out_specs=vmem,
        compiler_params=pltpu.CompilerParams(vmem_limit_bytes=4 << 20),
        name="assemble",
    )(value, *got)
    return out.reshape((-1,) + value.shape[1:])


def body(map_slabs, slot_slab, orient_index, slab_lo, slab_hi, tile_spectrum, prev_max, prev_sum, prev_sumsq):
    box, edge = map_slabs.shape[2], tile_spectrum.shape[1]
    devices = lax.axis_size("mic")
    bits = devices.bit_length() - 1
    rows = box * 4 // devices
    row, quad, quad_t = constants(box, edge)

    part = project(map_slabs, slot_slab, orient_index, slab_lo, slab_hi, rows)
    got = [swap(part, "proj", k) for k in range(1, lax.axis_size("proj"))]
    tile, _ = lax.optimization_barrier((tile_spectrum[0], part))
    th_real, th_imag = hermitian(tile)
    got, th_real, th_imag = lax.optimization_barrier((got, th_real, th_imag))
    pieces = total_of([part] + got)[None]
    for low in range(1, bits, 2):
        pieces = gather_group(pieces, low, min(2, bits - low))
    others = swap(pieces, "mic", 1)
    half = first_pair(pieces, th_real, th_imag, row, quad, quad_t)
    return tuple(second_pair(others, half, th_real, th_imag, row, quad, quad_t, prev_max, prev_sum, prev_sumsq))


def solution(mesh):
    tiles = P(("mic", "proj"), None, None)
    in_specs = (P("proj", None, None, None), P("proj"), P(), P(), P(), tiles, tiles, tiles, tiles)
    return jax.shard_map(body, mesh=mesh, in_specs=in_specs, out_specs=(tiles,) * 3, check_vma=False)
```

```python
import math

import jax
import jax.numpy as jnp
import ml_dtypes
import numpy as np
from jax import lax
from jax.experimental import pallas as pl
from jax.experimental.pallas import tpu as pltpu
from jax.sharding import PartitionSpec as P

SLAB_Z = 8
SLABS = 12
NORI = 256
MAX_SLOPE = 0.5
GOLDEN_ANGLE = 2.399963

F32 = jnp.float32
BF16 = jnp.bfloat16
TAP = jnp.int16


def phase_tables(edge):
    index = np.arange(edge, dtype=np.int64)
    turn = (index[:, None] * index[None, :] % edge).astype(np.float64) / edge
    scale = 1.0 / math.sqrt(edge)
    cos = (np.cos(2.0 * np.pi * turn) * scale).astype(np.float32)
    sin = (np.sin(2.0 * np.pi * turn) * scale).astype(np.float32)
    return cos.astype(ml_dtypes.bfloat16), sin.astype(ml_dtypes.bfloat16)


def class_order(edge):
    return np.concatenate([np.arange(r, edge, 4) for r in range(4)])


def constants(box, edge):
    cos, sin = phase_tables(edge)
    quarter = edge // 4
    order = class_order(edge)
    cg, sg = cos[order, :box].T, sin[order, :box].T
    row = np.block([[cg, -sg], [-sg, -cg]])
    quad = []
    for r in range(4):
        c, s = cos[r::4, :quarter], sin[r::4, :quarter]
        quad.append(np.block([[c, s], [-s, c]]))
    quad = np.stack(quad)
    quad_t = np.ascontiguousarray(quad.transpose(0, 2, 1))
    return tuple(jnp.asarray(x) for x in (row, quad, quad_t))


def dot(a, b):
    return jnp.dot(a, b, preferred_element_type=F32)


def tent(offsets):
    return jnp.maximum(0.0, 1.0 - jnp.abs(offsets))


def two_taps(index, shift):
    whole = jnp.floor(shift)
    frac = shift - whole
    tap = whole.astype(jnp.int32)
    tap, next_tap = tap.astype(index.dtype), (tap + 1).astype(index.dtype)
    low = jnp.full(index.shape, 1.0 - frac, F32).astype(BF16)
    high = jnp.full(index.shape, frac, F32).astype(BF16)
    zero = jnp.zeros(index.shape, BF16)
    return jnp.where(index == tap, low, jnp.where(index == next_tap, high, zero))


def project_kernel(
    rows, window, slot_hbm, orient_hbm, lo_hbm, hi_hbm, map_ref, out_ref,
    slabs, diff_y, right, acc, sems, slot_ref, orient_ref, lo_ref, hi_ref, param_sems, *shifted,
):
    slots, depth, box = map_ref.shape[0], map_ref.shape[1], map_ref.shape[2]
    half = box // 2
    me = lax.axis_index("mic")
    orient = (me % 2) * 2 + (me // 2) % 2
    first = (me // 4) * rows
    base = jnp.clip(first - 32, 0, box - window)
    base = pl.multiple_of(base // 16 * 16, 16)

    def fetch(i):
        return pltpu.make_async_copy(map_ref.at[i, :, pl.ds(base, window), :], slabs.at[i], sems.at[i])

    params = [
        pltpu.make_async_copy(src, dst, param_sems.at[n])
        for n, (src, dst) in enumerate(((slot_hbm, slot_ref), (orient_hbm, orient_ref), (lo_hbm, lo_ref), (hi_hbm, hi_ref)))
    ]
    for copy in params:
        copy.start()
    for i in range(slots):
        fetch(i).start()

    d = lax.broadcasted_iota(jnp.int32, (box, box), 0)
    c = lax.broadcasted_iota(jnp.int32, (box, box), 1)
    diff_y[...] = (d - c).astype(diff_y.dtype)
    acc[...] = jnp.zeros_like(acc)
    right[...] = jnp.zeros_like(right)
    for ref in shifted:
        ref[...] = jnp.zeros_like(ref)
    bands = ((slice(0, half + 32), slice(0, half)), (slice(half - 32, box), slice(half, box)))
    place = pl.ds(pl.multiple_of(base - first + 64, 16), window)

    for copy in params:
        copy.wait()
    step = jnp.full((8, 128), orient_ref[orient], jnp.int32).astype(F32)
    radius = MAX_SLOPE * jnp.sqrt((step + 0.5) / NORI)
    slope_x = jnp.max(radius * jnp.cos(GOLDEN_ANGLE * step))
    slope_y = jnp.max(radius * jnp.sin(GOLDEN_ANGLE * step))
    low, high = lo_ref[orient], hi_ref[orient]

    for i in range(slots):
        fetch(i).wait()
        slab = slot_ref[i]

        @pl.when((slab >= low) & (slab < high))
        def _():
            depths = [(slab * depth + j).astype(F32) - (SLABS * SLAB_Z - 1) / 2.0 for j in range(depth)]

            def across(j):
                for ds, cs in bands:
                    right[j, ds, cs] = two_taps(diff_y[ds, cs], slope_y * depths[j])
                moved = dot(slabs[i, j], right[j])
                shifted[2 * j][place, :] = moved[:, :half]
                shifted[2 * j + 1][place, :] = moved[:, half:]

            def down(j, total):
                shift = slope_x * depths[j]
                whole = jnp.floor(shift)
                start = whole.astype(jnp.int32) + 64
                near = jnp.full((1, half), 1.0 - (shift - whole), F32).astype(BF16).astype(F32)
                far = jnp.full((1, half), shift - whole, F32).astype(BF16).astype(F32)
                return [
                    total[n] + near * shifted[2 * j + n][pl.ds(start, rows), :] + far * shifted[2 * j + n][pl.ds(start + 1, rows), :]
                    for n in range(2)
                ]

            total = [acc[0], acc[1]]
            across(0)
            for j in range(depth):
                if j + 1 < depth:
                    across(j + 1)
                total = down(j, total)
            acc[0], acc[1] = total

    out_ref[:, :half] = acc[0].astype(BF16)
    out_ref[:, half:] = acc[1].astype(BF16)


def project(map_slabs, slot_slab, orient_index, slab_lo, slab_hi, rows):
    slots, depth, box = map_slabs.shape[:3]
    blocks = box // rows
    window = min(box, rows + 32 * min(2, blocks - 1))
    args = [pltpu.with_memory_space_constraint(x, pltpu.HBM) for x in (slot_slab, orient_index, slab_lo, slab_hi, map_slabs)]
    return pl.pallas_call(
        lambda *refs: project_kernel(rows, window, *refs),
        out_shape=jax.ShapeDtypeStruct((rows, box), BF16),
        in_specs=[pl.BlockSpec(memory_space=pltpu.HBM)] * 5,
        out_specs=pl.BlockSpec(memory_space=pltpu.VMEM),
        scratch_shapes=[
            pltpu.VMEM((slots, depth, window, box), BF16),
            pltpu.VMEM((box, box), TAP),
            pltpu.VMEM((depth, box, box), BF16),
            pltpu.VMEM((2, rows, box // 2), F32),
            pltpu.SemaphoreType.DMA((slots,)),
            pltpu.SMEM(slot_slab.shape, jnp.int32),
            pltpu.SMEM(orient_index.shape, jnp.int32),
            pltpu.SMEM(orient_index.shape, jnp.int32),
            pltpu.SMEM(orient_index.shape, jnp.int32),
            pltpu.SemaphoreType.DMA((4,)),
        ]
        + [pltpu.VMEM((window + 96, box // 2), F32)] * (2 * depth),
        compiler_params=pltpu.CompilerParams(vmem_limit_bytes=16 << 20),
        name="project",
    )(*args)


def total_kernel(*refs):
    total = refs[0][...].astype(F32)
    for ref in refs[1:-1]:
        total = total + ref[...].astype(F32)
    refs[-1][...] = total.astype(BF16)


def total_of(parts):
    vmem = pl.BlockSpec(memory_space=pltpu.VMEM)
    return pl.pallas_call(
        total_kernel,
        out_shape=jax.ShapeDtypeStruct(parts[0].shape, BF16),
        in_specs=[vmem] * len(parts),
        out_specs=vmem,
        compiler_params=pltpu.CompilerParams(vmem_limit_bytes=2 << 20),
        name="total",
    )(*parts)


def hermitian_kernel(tile_ref, real_ref, imag_ref, picked):
    edge = real_ref.shape[0]
    quarter = edge // 4

    def pick(dim):
        shape = (2 * edge, edge) if dim == 0 else (edge, 2 * edge)
        place = lax.broadcasted_iota(jnp.int32, shape, dim)
        freq = lax.broadcasted_iota(jnp.int32, shape, 1 - dim)
        inner = place & (edge - 1)
        wanted = 4 * (inner & (quarter - 1)) + inner // quarter
        wanted = jnp.where(place < edge, wanted, (edge - wanted) & (edge - 1))
        return freq == wanted

    rows = jnp.where(pick(0), 1.0, 0.0).astype(BF16)
    picked[...] = dot(rows, tile_ref[...]).astype(BF16)
    cols = jnp.where(pick(1), 0.5, 0.0).astype(BF16)
    cols = jnp.concatenate([cols[:, :edge], cols[:, edge:]], axis=0)
    real = jnp.concatenate([picked[:edge, :edge], picked[edge:, :edge]], axis=1)
    real_ref[...] = dot(real, cols)
    imag = jnp.concatenate([picked[:edge, edge:], -picked[edge:, edge:]], axis=1)
    imag_ref[...] = dot(imag, cols)


def hermitian(tile):
    edge = tile.shape[0]
    vmem = pl.BlockSpec(memory_space=pltpu.VMEM)
    return pl.pallas_call(
        hermitian_kernel,
        out_shape=[jax.ShapeDtypeStruct((edge, edge), F32)] * 2,
        in_specs=[vmem],
        out_specs=[vmem] * 2,
        scratch_shapes=[pltpu.VMEM((2 * edge, 2 * edge), BF16)],
        compiler_params=pltpu.CompilerParams(vmem_limit_bytes=16 << 20),
        cost_estimate=pl.CostEstimate(flops=8 * edge**3 * 2, bytes_accessed=12 * edge * edge, transcendentals=0),
        name="hermitian",
    )(tile)


def half_transform(pieces_ref, real_ref, imag_ref, row_ref, quad_ref, quadt_ref, stack, half):
    count, rows, box = pieces_ref.shape
    edge = real_ref.shape[0]
    quarter = edge // 4
    for q in range(count):
        stack[(q // 2) * rows : (q // 2 + 1) * rows, (q % 2) * box : (q % 2 + 1) * box] = pieces_ref[q]
    width = 2 * quarter
    inputs = {}
    for gh in range(edge // width):
        rr = dot(stack[...], row_ref[:, gh * width : (gh + 1) * width])
        ri = dot(stack[...], row_ref[:, edge + gh * width : edge + (gh + 1) * width])
        r0, r1 = rr[:quarter], rr[quarter:]
        i0, i1 = ri[:quarter], ri[quarter:]
        for r, pair in enumerate(((r0 + r1, i0 + i1), (r0 + i1, i0 - r1), (r0 - r1, i0 - i1), (r0 - i1, i0 + r1))):
            inputs[gh, r] = jnp.concatenate(pair, axis=0).astype(BF16)
    items = [(gh, r) for gh in range(edge // width) for r in range(4)]
    parts = {}

    def spectrum(gh, r):
        return dot(quad_ref[r], inputs[gh, r])

    def back(gh, r, spec):
        cols = slice(gh * width, (gh + 1) * width)
        sr, si = spec[:quarter], spec[quarter:]
        fr = slice(r * quarter, (r + 1) * quarter)
        tr, ti = real_ref[fr, cols], imag_ref[fr, cols]
        product = jnp.concatenate([tr * sr + ti * si, ti * sr - tr * si], axis=0).astype(BF16)
        parts[gh, r] = dot(quadt_ref[r], product)

    def combine(gh):
        part = [parts[gh, r] for r in range(4)]
        ar, ai = part[0][:quarter] + part[2][:quarter], part[0][quarter:] + part[2][quarter:]
        br, bi = part[0][:quarter] - part[2][:quarter], part[0][quarter:] - part[2][quarter:]
        cr, ci = part[1][:quarter] + part[3][:quarter], part[1][quarter:] + part[3][quarter:]
        dr, di = part[1][:quarter] - part[3][:quarter], part[1][quarter:] - part[3][quarter:]
        outs = ((ar + cr, ai + ci), (br - di, bi + dr), (ar - cr, ai - ci), (br + di, bi - dr))
        for k in range(4):
            xs = slice(k * quarter, (k + 1) * quarter)
            hr, hi = outs[k][0].astype(BF16), outs[k][1].astype(BF16)
            for t in range(2):
                lanes = slice(t * quarter, (t + 1) * quarter)
                start = (2 * gh + t) * width
                half[xs, start : start + quarter] = hr[:, lanes]
                half[xs, start + quarter : start + width] = hi[:, lanes]

    ahead = 1
    specs = {item: spectrum(*item) for item in items[:ahead]}
    for n, item in enumerate(items):
        if n + ahead < len(items):
            specs[items[n + ahead]] = spectrum(*items[n + ahead])
        back(*item, specs.pop(item))
        if n % 4 == 1 and n > 4:
            combine(n // 4 - 1)
    combine(len(items) // 4 - 1)


def first_kernel(pieces_ref, real_ref, imag_ref, row_ref, quad_ref, quadt_ref, half_ref, stack):
    half_transform(pieces_ref, real_ref, imag_ref, row_ref, quad_ref, quadt_ref, stack, half_ref)


def first_pair(pieces, th_real, th_imag, row, quad, quad_t):
    box, edge = pieces.shape[2], th_real.shape[0]
    vmem = pl.BlockSpec(memory_space=pltpu.VMEM)
    return pl.pallas_call(
        first_kernel,
        out_shape=jax.ShapeDtypeStruct((edge, 2 * edge), BF16),
        in_specs=[vmem] * 6,
        out_specs=vmem,
        scratch_shapes=[pltpu.VMEM((box, 2 * box), BF16)],
        compiler_params=pltpu.CompilerParams(vmem_limit_bytes=12 << 20),
        cost_estimate=pl.CostEstimate(flops=6 * edge**3, bytes_accessed=12 * edge * edge, transcendentals=0),
        name="first_pair",
    )(pieces, th_real, th_imag, row, quad, quad_t)


def columns_of(half, quad_ref, quarter):
    width = 2 * quarter
    return [dot(half[:, s * width : (s + 1) * width], quad_ref[s]) for s in range(4)]


def scores_of(f, quarter):
    re = [x[:, :quarter] for x in f]
    im = [x[:, quarter:] for x in f]
    ar, ai, br, bi = re[0] + re[2], im[0] + im[2], re[0] - re[2], im[0] - im[2]
    cr, ci, dr, di = re[1] + re[3], im[1] + im[3], re[1] - re[3], im[1] - im[3]
    return ((ar + cr, ai + ci), (br - di, bi + dr), (ar - cr, ai - ci), (br + di, bi - dr))


def second_kernel(
    block, pieces_ref, half_ref, real_ref, imag_ref, row_ref, quad_ref, quadt_ref, max_ref, sum_ref, sq_ref,
    best_ref, total_ref, square_ref, stack, other, best_out, total_out, square_out, sems,
):
    edge = max_ref.shape[2]
    quarter = edge // 4
    half_transform(pieces_ref, real_ref, imag_ref, row_ref, quad_ref, quadt_ref, stack, other)
    copies = []
    steps = edge // block

    def columns(step):
        xs = slice(step * block, (step + 1) * block)
        return columns_of(half_ref[xs, :], quad_ref, quarter), columns_of(other[xs, :], quad_ref, quarter)

    ready = columns(0)
    for step in range(steps):
        xs = slice(step * block, (step + 1) * block)
        one, two = (scores_of(x, quarter) for x in ready)
        if step + 1 < steps:
            ready = columns(step + 1)
        for k in range(4):
            ys = slice(k * quarter, (k + 1) * quarter)
            best, total, square = max_ref[0, xs, ys], sum_ref[0, xs, ys], sq_ref[0, xs, ys]
            for score in (*one[k], *two[k]):
                best = jnp.maximum(best, score)
                total = total + score
                square = square + score * score
            best_out[xs, ys] = best
            total_out[xs, ys] = total
            square_out[xs, ys] = square
        for n, (src, dst) in enumerate(((best_out, best_ref), (total_out, total_ref), (square_out, square_ref))):
            copy = pltpu.make_async_copy(src.at[xs, :], dst.at[0, xs, :], sems.at[step, n])
            copy.start()
            copies.append(copy)
    for copy in copies:
        copy.wait()


def second_pair(pieces, half, th_real, th_imag, row, quad, quad_t, prev_max, prev_sum, prev_sumsq):
    box, edge = pieces.shape[2], th_real.shape[0]
    block = edge // 4
    vmem = pl.BlockSpec(memory_space=pltpu.VMEM)
    return pl.pallas_call(
        lambda *refs: second_kernel(block, *refs),
        out_shape=[jax.ShapeDtypeStruct(prev_max.shape, F32)] * 3,
        in_specs=[vmem] * 10,
        out_specs=[pl.BlockSpec(memory_space=pltpu.HBM)] * 3,
        scratch_shapes=[
            pltpu.VMEM((box, 2 * box), BF16),
            pltpu.VMEM((edge, 2 * edge), BF16),
            pltpu.VMEM((edge, edge), F32),
            pltpu.VMEM((edge, edge), F32),
            pltpu.VMEM((edge, edge), F32),
            pltpu.SemaphoreType.DMA((edge // block, 3)),
        ],
        compiler_params=pltpu.CompilerParams(vmem_limit_bytes=16 << 20),
        cost_estimate=pl.CostEstimate(flops=10 * edge**3, bytes_accessed=40 * edge * edge, transcendentals=0),
        name="second_pair",
    )(pieces, half, th_real, th_imag, row, quad, quad_t, prev_max, prev_sum, prev_sumsq)


def swap(value, axis, offset):
    return lax.ppermute(value, axis, [(i, i ^ offset) for i in range(lax.axis_size(axis))])


def assemble_kernel(low_bit, bits, *refs):
    mine = (lax.axis_index("mic") >> low_bit) & ((1 << bits) - 1)
    for k, ref in enumerate(refs[:-1]):
        refs[-1][mine ^ k] = ref[...]


def gather_group(value, low_bit, bits):
    got = [swap(value, "mic", k << low_bit) for k in range(1, 1 << bits)]
    vmem = pl.BlockSpec(memory_space=pltpu.VMEM)
    out = pl.pallas_call(
        lambda *refs: assemble_kernel(low_bit, bits, *refs),
        out_shape=jax.ShapeDtypeStruct((1 << bits,) + value.shape, value.dtype),
        in_specs=[vmem] * (1 << bits),
        out_specs=vmem,
        compiler_params=pltpu.CompilerParams(vmem_limit_bytes=4 << 20),
        name="assemble",
    )(value, *got)
    return out.reshape((-1,) + value.shape[1:])


def body(map_slabs, slot_slab, orient_index, slab_lo, slab_hi, tile_spectrum, prev_max, prev_sum, prev_sumsq):
    box, edge = map_slabs.shape[2], tile_spectrum.shape[1]
    devices = lax.axis_size("mic")
    bits = devices.bit_length() - 1
    rows = box * 4 // devices
    row, quad, quad_t = constants(box, edge)

    part = project(map_slabs, slot_slab, orient_index, slab_lo, slab_hi, rows)
    got = [swap(part, "proj", k) for k in range(1, lax.axis_size("proj"))]
    tile, _ = lax.optimization_barrier((tile_spectrum[0], part))
    th_real, th_imag = hermitian(tile)
    got, th_real, th_imag = lax.optimization_barrier((got, th_real, th_imag))
    pieces = total_of([part] + got)[None]
    for low in range(1, bits, 2):
        pieces = gather_group(pieces, low, min(2, bits - low))
    others = swap(pieces, "mic", 1)
    half = first_pair(pieces, th_real, th_imag, row, quad, quad_t)
    return tuple(second_pair(others, half, th_real, th_imag, row, quad, quad_t, prev_max, prev_sum, prev_sumsq))


def solution(mesh):
    tiles = P(("mic", "proj"), None, None)
    in_specs = (P("proj", None, None, None), P("proj"), P(), P(), P(), tiles, tiles, tiles, tiles)
    return jax.shard_map(body, mesh=mesh, in_specs=in_specs, out_specs=(tiles,) * 3, check_vma=False)
```

```python
import math

import jax
import jax.numpy as jnp
import ml_dtypes
import numpy as np
from jax import lax
from jax.experimental import pallas as pl
from jax.experimental.pallas import tpu as pltpu
from jax.sharding import PartitionSpec as P

SLAB_Z = 8
SLABS = 12
NORI = 256
MAX_SLOPE = 0.5
GOLDEN_ANGLE = 2.399963

F32 = jnp.float32
BF16 = jnp.bfloat16
TAP = jnp.int16


def phase_tables(edge):
    index = np.arange(edge, dtype=np.int64)
    turn = (index[:, None] * index[None, :] % edge).astype(np.float64) / edge
    scale = 1.0 / math.sqrt(edge)
    cos = (np.cos(2.0 * np.pi * turn) * scale).astype(np.float32)
    sin = (np.sin(2.0 * np.pi * turn) * scale).astype(np.float32)
    return cos.astype(ml_dtypes.bfloat16), sin.astype(ml_dtypes.bfloat16)


def class_order(edge):
    return np.concatenate([np.arange(r, edge, 4) for r in range(4)])


def constants(box, edge):
    cos, sin = phase_tables(edge)
    quarter = edge // 4
    order = class_order(edge)
    cg, sg = cos[order, :box].T, sin[order, :box].T
    row = np.block([[cg, -sg], [-sg, -cg]])
    quad = []
    for r in range(4):
        c, s = cos[r::4, :quarter], sin[r::4, :quarter]
        quad.append(np.block([[c, s], [-s, c]]))
    quad = np.stack(quad)
    quad_t = np.ascontiguousarray(quad.transpose(0, 2, 1))
    return tuple(jnp.asarray(x) for x in (row, quad, quad_t))


def dot(a, b):
    return jnp.dot(a, b, preferred_element_type=F32)


def tent(offsets):
    return jnp.maximum(0.0, 1.0 - jnp.abs(offsets))


def two_taps(index, shift):
    whole = jnp.floor(shift)
    frac = shift - whole
    tap = whole.astype(jnp.int32)
    tap, next_tap = tap.astype(index.dtype), (tap + 1).astype(index.dtype)
    low = jnp.full(index.shape, 1.0 - frac, F32).astype(BF16)
    high = jnp.full(index.shape, frac, F32).astype(BF16)
    zero = jnp.zeros(index.shape, BF16)
    return jnp.where(index == tap, low, jnp.where(index == next_tap, high, zero))


def project_kernel(
    rows, window, slot_hbm, orient_hbm, lo_hbm, hi_hbm, map_ref, out_ref,
    slabs, diff_y, right, acc, sems, slot_ref, orient_ref, lo_ref, hi_ref, param_sems, *shifted,
):
    slots, depth, box = map_ref.shape[0], map_ref.shape[1], map_ref.shape[2]
    half = box // 2
    me = lax.axis_index("mic")
    orient = (me % 2) * 2 + (me // 2) % 2
    first = (me // 4) * rows
    base = jnp.clip(first - 32, 0, box - window)
    base = pl.multiple_of(base // 16 * 16, 16)

    def fetch(i):
        return pltpu.make_async_copy(map_ref.at[i, :, pl.ds(base, window), :], slabs.at[i], sems.at[i])

    params = [
        pltpu.make_async_copy(src, dst, param_sems.at[n])
        for n, (src, dst) in enumerate(((slot_hbm, slot_ref), (orient_hbm, orient_ref), (lo_hbm, lo_ref), (hi_hbm, hi_ref)))
    ]
    for copy in params:
        copy.start()
    for i in range(slots):
        fetch(i).start()

    d = lax.broadcasted_iota(jnp.int32, (box, box), 0)
    c = lax.broadcasted_iota(jnp.int32, (box, box), 1)
    diff_y[...] = (d - c).astype(diff_y.dtype)
    acc[...] = jnp.zeros_like(acc)
    right[...] = jnp.zeros_like(right)
    for ref in shifted:
        ref[...] = jnp.zeros_like(ref)
    bands = ((slice(0, half + 32), slice(0, half)), (slice(half - 32, box), slice(half, box)))
    place = pl.ds(pl.multiple_of(base - first + 64, 16), window)

    for copy in params:
        copy.wait()
    step = jnp.full((8, 128), orient_ref[orient], jnp.int32).astype(F32)
    radius = MAX_SLOPE * jnp.sqrt((step + 0.5) / NORI)
    slope_x = jnp.max(radius * jnp.cos(GOLDEN_ANGLE * step))
    slope_y = jnp.max(radius * jnp.sin(GOLDEN_ANGLE * step))
    low, high = lo_ref[orient], hi_ref[orient]

    for i in range(slots):
        fetch(i).wait()
        slab = slot_ref[i]

        @pl.when((slab >= low) & (slab < high))
        def _():
            depths = [(slab * depth + j).astype(F32) - (SLABS * SLAB_Z - 1) / 2.0 for j in range(depth)]

            def across(j):
                for ds, cs in bands:
                    right[j, ds, cs] = two_taps(diff_y[ds, cs], slope_y * depths[j])
                moved = dot(slabs[i, j], right[j])
                shifted[2 * j][place, :] = moved[:, :half]
                shifted[2 * j + 1][place, :] = moved[:, half:]

            def down(j, total):
                shift = slope_x * depths[j]
                whole = jnp.floor(shift)
                start = whole.astype(jnp.int32) + 64
                near = jnp.full((1, half), 1.0 - (shift - whole), F32).astype(BF16).astype(F32)
                far = jnp.full((1, half), shift - whole, F32).astype(BF16).astype(F32)
                return [
                    total[n] + near * shifted[2 * j + n][pl.ds(start, rows), :] + far * shifted[2 * j + n][pl.ds(start + 1, rows), :]
                    for n in range(2)
                ]

            total = [acc[0], acc[1]]
            across(0)
            for j in range(depth):
                if j + 1 < depth:
                    across(j + 1)
                total = down(j, total)
            acc[0], acc[1] = total

    out_ref[:, :half] = acc[0].astype(BF16)
    out_ref[:, half:] = acc[1].astype(BF16)


def project(map_slabs, slot_slab, orient_index, slab_lo, slab_hi, rows):
    slots, depth, box = map_slabs.shape[:3]
    blocks = box // rows
    window = min(box, rows + 32 * min(2, blocks - 1))
    args = [pltpu.with_memory_space_constraint(x, pltpu.HBM) for x in (slot_slab, orient_index, slab_lo, slab_hi, map_slabs)]
    return pl.pallas_call(
        lambda *refs: project_kernel(rows, window, *refs),
        out_shape=jax.ShapeDtypeStruct((rows, box), BF16),
        in_specs=[pl.BlockSpec(memory_space=pltpu.HBM)] * 5,
        out_specs=pl.BlockSpec(memory_space=pltpu.VMEM),
        scratch_shapes=[
            pltpu.VMEM((slots, depth, window, box), BF16),
            pltpu.VMEM((box, box), TAP),
            pltpu.VMEM((depth, box, box), BF16),
            pltpu.VMEM((2, rows, box // 2), F32),
            pltpu.SemaphoreType.DMA((slots,)),
            pltpu.SMEM(slot_slab.shape, jnp.int32),
            pltpu.SMEM(orient_index.shape, jnp.int32),
            pltpu.SMEM(orient_index.shape, jnp.int32),
            pltpu.SMEM(orient_index.shape, jnp.int32),
            pltpu.SemaphoreType.DMA((4,)),
        ]
        + [pltpu.VMEM((window + 96, box // 2), F32)] * (2 * depth),
        compiler_params=pltpu.CompilerParams(vmem_limit_bytes=16 << 20),
        name="project",
    )(*args)


def total_kernel(*refs):
    total = refs[0][...].astype(F32)
    for ref in refs[1:-1]:
        total = total + ref[...].astype(F32)
    refs[-1][...] = total.astype(BF16)


def total_of(parts):
    vmem = pl.BlockSpec(memory_space=pltpu.VMEM)
    return pl.pallas_call(
        total_kernel,
        out_shape=jax.ShapeDtypeStruct(parts[0].shape, BF16),
        in_specs=[vmem] * len(parts),
        out_specs=vmem,
        compiler_params=pltpu.CompilerParams(vmem_limit_bytes=2 << 20),
        name="total",
    )(*parts)


def hermitian_kernel(tile_ref, real_ref, imag_ref, picked):
    edge = real_ref.shape[0]
    quarter = edge // 4

    def pick(dim):
        shape = (2 * edge, edge) if dim == 0 else (edge, 2 * edge)
        place = lax.broadcasted_iota(jnp.int32, shape, dim)
        freq = lax.broadcasted_iota(jnp.int32, shape, 1 - dim)
        inner = place & (edge - 1)
        wanted = 4 * (inner & (quarter - 1)) + inner // quarter
        wanted = jnp.where(place < edge, wanted, (edge - wanted) & (edge - 1))
        return freq == wanted

    rows = jnp.where(pick(0), 1.0, 0.0).astype(BF16)
    picked[...] = dot(rows, tile_ref[...]).astype(BF16)
    cols = jnp.where(pick(1), 0.5, 0.0).astype(BF16)
    cols = jnp.concatenate([cols[:, :edge], cols[:, edge:]], axis=0)
    real = jnp.concatenate([picked[:edge, :edge], picked[edge:, :edge]], axis=1)
    real_ref[...] = dot(real, cols)
    imag = jnp.concatenate([picked[:edge, edge:], -picked[edge:, edge:]], axis=1)
    imag_ref[...] = dot(imag, cols)


def hermitian(tile):
    edge = tile.shape[0]
    vmem = pl.BlockSpec(memory_space=pltpu.VMEM)
    return pl.pallas_call(
        hermitian_kernel,
        out_shape=[jax.ShapeDtypeStruct((edge, edge), F32)] * 2,
        in_specs=[vmem],
        out_specs=[vmem] * 2,
        scratch_shapes=[pltpu.VMEM((2 * edge, 2 * edge), BF16)],
        compiler_params=pltpu.CompilerParams(vmem_limit_bytes=16 << 20),
        cost_estimate=pl.CostEstimate(flops=8 * edge**3 * 2, bytes_accessed=12 * edge * edge, transcendentals=0),
        name="hermitian",
    )(tile)


def half_transform(pieces_ref, real_ref, imag_ref, row_ref, quad_ref, quadt_ref, stack, half):
    count, rows, box = pieces_ref.shape
    edge = real_ref.shape[0]
    quarter = edge // 4
    for q in range(count):
        stack[(q // 2) * rows : (q // 2 + 1) * rows, (q % 2) * box : (q % 2 + 1) * box] = pieces_ref[q]
    width = 2 * quarter
    inputs = {}
    rows_of = {}

    def row(gh, part):
        start = part * edge + gh * width
        rows_of[gh, part] = dot(stack[...], row_ref[:, start : start + width])

    def fold(gh):
        rr, ri = rows_of[gh, 0], rows_of[gh, 1]
        r0, r1 = rr[:quarter], rr[quarter:]
        i0, i1 = ri[:quarter], ri[quarter:]
        for r, pair in enumerate(((r0 + r1, i0 + i1), (r0 + i1, i0 - r1), (r0 - r1, i0 - i1), (r0 - i1, i0 + r1))):
            inputs[gh, r] = jnp.concatenate(pair, axis=0).astype(BF16)

    items = [(gh, r) for gh in range(edge // width) for r in range(4)]
    parts = {}

    def spectrum(gh, r):
        return dot(quad_ref[r], inputs[gh, r])

    def back(gh, r, spec):
        cols = slice(gh * width, (gh + 1) * width)
        sr, si = spec[:quarter], spec[quarter:]
        fr = slice(r * quarter, (r + 1) * quarter)
        tr, ti = real_ref[fr, cols], imag_ref[fr, cols]
        product = jnp.concatenate([tr * sr + ti * si, ti * sr - tr * si], axis=0).astype(BF16)
        parts[gh, r] = dot(quadt_ref[r], product)

    def combine(gh):
        part = [parts[gh, r] for r in range(4)]
        ar, ai = part[0][:quarter] + part[2][:quarter], part[0][quarter:] + part[2][quarter:]
        br, bi = part[0][:quarter] - part[2][:quarter], part[0][quarter:] - part[2][quarter:]
        cr, ci = part[1][:quarter] + part[3][:quarter], part[1][quarter:] + part[3][quarter:]
        dr, di = part[1][:quarter] - part[3][:quarter], part[1][quarter:] - part[3][quarter:]
        outs = ((ar + cr, ai + ci), (br - di, bi + dr), (ar - cr, ai - ci), (br + di, bi - dr))
        for k in range(4):
            xs = slice(k * quarter, (k + 1) * quarter)
            hr, hi = outs[k][0].astype(BF16), outs[k][1].astype(BF16)
            for t in range(2):
                lanes = slice(t * quarter, (t + 1) * quarter)
                start = (2 * gh + t) * width
                half[xs, start : start + quarter] = hr[:, lanes]
                half[xs, start + quarter : start + width] = hi[:, lanes]

    specs = {}
    for token in "R0 R1 R2 R3 U0 S0 S1 S2 S3 U1 S4 B0 S5 B1 S6 B2 S7 B3 B4 B5 C0 B6 B7 C1".split():
        act, n = token[0], int(token[1])
        if act == "R":
            row(n // 2, n % 2)
        elif act == "U":
            fold(n)
        elif act == "S":
            specs[n] = spectrum(*items[n])
        elif act == "B":
            back(*items[n], specs.pop(n))
        else:
            combine(n)


def first_kernel(pieces_ref, real_ref, imag_ref, row_ref, quad_ref, quadt_ref, half_ref, stack):
    half_transform(pieces_ref, real_ref, imag_ref, row_ref, quad_ref, quadt_ref, stack, half_ref)


def first_pair(pieces, th_real, th_imag, row, quad, quad_t):
    box, edge = pieces.shape[2], th_real.shape[0]
    vmem = pl.BlockSpec(memory_space=pltpu.VMEM)
    return pl.pallas_call(
        first_kernel,
        out_shape=jax.ShapeDtypeStruct((edge, 2 * edge), BF16),
        in_specs=[vmem] * 6,
        out_specs=vmem,
        scratch_shapes=[pltpu.VMEM((box, 2 * box), BF16)],
        compiler_params=pltpu.CompilerParams(vmem_limit_bytes=12 << 20),
        cost_estimate=pl.CostEstimate(flops=6 * edge**3, bytes_accessed=12 * edge * edge, transcendentals=0),
        name="first_pair",
    )(pieces, th_real, th_imag, row, quad, quad_t)


def columns_of(half, quad_ref, quarter):
    width = 2 * quarter
    return [dot(half[:, s * width : (s + 1) * width], quad_ref[s]) for s in range(4)]


def scores_of(f, quarter):
    re = [x[:, :quarter] for x in f]
    im = [x[:, quarter:] for x in f]
    ar, ai, br, bi = re[0] + re[2], im[0] + im[2], re[0] - re[2], im[0] - im[2]
    cr, ci, dr, di = re[1] + re[3], im[1] + im[3], re[1] - re[3], im[1] - im[3]
    return ((ar + cr, ai + ci), (br - di, bi + dr), (ar - cr, ai - ci), (br + di, bi - dr))


def second_kernel(
    block, pieces_ref, half_ref, real_ref, imag_ref, row_ref, quad_ref, quadt_ref, max_ref, sum_ref, sq_ref,
    best_ref, total_ref, square_ref, stack, other, best_out, total_out, square_out, sems,
):
    edge = max_ref.shape[2]
    quarter = edge // 4
    half_transform(pieces_ref, real_ref, imag_ref, row_ref, quad_ref, quadt_ref, stack, other)
    copies = []
    steps = edge // block

    def columns(step):
        xs = slice(step * block, (step + 1) * block)
        return columns_of(half_ref[xs, :], quad_ref, quarter), columns_of(other[xs, :], quad_ref, quarter)

    ready = columns(0)
    for step in range(steps):
        xs = slice(step * block, (step + 1) * block)
        one, two = (scores_of(x, quarter) for x in ready)
        if step + 1 < steps:
            ready = columns(step + 1)
        for k in range(4):
            ys = slice(k * quarter, (k + 1) * quarter)
            best, total, square = max_ref[0, xs, ys], sum_ref[0, xs, ys], sq_ref[0, xs, ys]
            for score in (*one[k], *two[k]):
                best = jnp.maximum(best, score)
                total = total + score
                square = square + score * score
            best_out[xs, ys] = best
            total_out[xs, ys] = total
            square_out[xs, ys] = square
        for n, (src, dst) in enumerate(((best_out, best_ref), (total_out, total_ref), (square_out, square_ref))):
            copy = pltpu.make_async_copy(src.at[xs, :], dst.at[0, xs, :], sems.at[step, n])
            copy.start()
            copies.append(copy)
    for copy in copies:
        copy.wait()


def second_pair(pieces, half, th_real, th_imag, row, quad, quad_t, prev_max, prev_sum, prev_sumsq):
    box, edge = pieces.shape[2], th_real.shape[0]
    block = edge // 4
    vmem = pl.BlockSpec(memory_space=pltpu.VMEM)
    return pl.pallas_call(
        lambda *refs: second_kernel(block, *refs),
        out_shape=[jax.ShapeDtypeStruct(prev_max.shape, F32)] * 3,
        in_specs=[vmem] * 10,
        out_specs=[pl.BlockSpec(memory_space=pltpu.HBM)] * 3,
        scratch_shapes=[
            pltpu.VMEM((box, 2 * box), BF16),
            pltpu.VMEM((edge, 2 * edge), BF16),
            pltpu.VMEM((edge, edge), F32),
            pltpu.VMEM((edge, edge), F32),
            pltpu.VMEM((edge, edge), F32),
            pltpu.SemaphoreType.DMA((edge // block, 3)),
        ],
        compiler_params=pltpu.CompilerParams(vmem_limit_bytes=16 << 20),
        cost_estimate=pl.CostEstimate(flops=10 * edge**3, bytes_accessed=40 * edge * edge, transcendentals=0),
        name="second_pair",
    )(pieces, half, th_real, th_imag, row, quad, quad_t, prev_max, prev_sum, prev_sumsq)


def swap(value, axis, offset):
    return lax.ppermute(value, axis, [(i, i ^ offset) for i in range(lax.axis_size(axis))])


def assemble_kernel(low_bit, bits, *refs):
    mine = (lax.axis_index("mic") >> low_bit) & ((1 << bits) - 1)
    for k, ref in enumerate(refs[:-1]):
        refs[-1][mine ^ k] = ref[...]


def gather_group(value, low_bit, bits):
    got = [swap(value, "mic", k << low_bit) for k in range(1, 1 << bits)]
    vmem = pl.BlockSpec(memory_space=pltpu.VMEM)
    out = pl.pallas_call(
        lambda *refs: assemble_kernel(low_bit, bits, *refs),
        out_shape=jax.ShapeDtypeStruct((1 << bits,) + value.shape, value.dtype),
        in_specs=[vmem] * (1 << bits),
        out_specs=vmem,
        compiler_params=pltpu.CompilerParams(vmem_limit_bytes=4 << 20),
        name="assemble",
    )(value, *got)
    return out.reshape((-1,) + value.shape[1:])


def body(map_slabs, slot_slab, orient_index, slab_lo, slab_hi, tile_spectrum, prev_max, prev_sum, prev_sumsq):
    box, edge = map_slabs.shape[2], tile_spectrum.shape[1]
    devices = lax.axis_size("mic")
    bits = devices.bit_length() - 1
    rows = box * 4 // devices
    row, quad, quad_t = constants(box, edge)

    part = project(map_slabs, slot_slab, orient_index, slab_lo, slab_hi, rows)
    got = [swap(part, "proj", k) for k in sorted(range(1, lax.axis_size("proj")), key=lambda k: (k & (k - 1) == 0 and k > 1, k))]
    tile, _ = lax.optimization_barrier((tile_spectrum[0], part))
    th_real, th_imag = hermitian(tile)
    got, th_real, th_imag = lax.optimization_barrier((got, th_real, th_imag))
    pieces = total_of([part] + got)[None]
    for low in range(1, bits, 2):
        pieces = gather_group(pieces, low, min(2, bits - low))
    others = swap(pieces, "mic", 1)
    half = first_pair(pieces, th_real, th_imag, row, quad, quad_t)
    return tuple(second_pair(others, half, th_real, th_imag, row, quad, quad_t, prev_max, prev_sum, prev_sumsq))


def solution(mesh):
    tiles = P(("mic", "proj"), None, None)
    in_specs = (P("proj", None, None, None), P("proj"), P(), P(), P(), tiles, tiles, tiles, tiles)
    return jax.shard_map(body, mesh=mesh, in_specs=in_specs, out_specs=(tiles,) * 3, check_vma=False)
```

```python
import math

import jax
import jax.numpy as jnp
import ml_dtypes
import numpy as np
from jax import lax
from jax.experimental import pallas as pl
from jax.experimental.pallas import tpu as pltpu
from jax.sharding import PartitionSpec as P

SLAB_Z = 8
SLABS = 12
NORI = 256
MAX_SLOPE = 0.5
GOLDEN_ANGLE = 2.399963

F32 = jnp.float32
BF16 = jnp.bfloat16
TAP = jnp.int16


def phase_tables(edge):
    index = np.arange(edge, dtype=np.int64)
    turn = (index[:, None] * index[None, :] % edge).astype(np.float64) / edge
    scale = 1.0 / math.sqrt(edge)
    cos = (np.cos(2.0 * np.pi * turn) * scale).astype(np.float32)
    sin = (np.sin(2.0 * np.pi * turn) * scale).astype(np.float32)
    return cos.astype(ml_dtypes.bfloat16), sin.astype(ml_dtypes.bfloat16)


def class_order(edge):
    return np.concatenate([np.arange(r, edge, 4) for r in range(4)])


def constants(box, edge):
    cos, sin = phase_tables(edge)
    quarter = edge // 4
    order = class_order(edge)
    cg, sg = cos[order, :box].T, sin[order, :box].T
    row = np.block([[cg, -sg], [-sg, -cg]])
    quad = []
    for r in range(4):
        c, s = cos[r::4, :quarter], sin[r::4, :quarter]
        quad.append(np.block([[c, s], [-s, c]]))
    quad = np.stack(quad)
    quad_t = np.ascontiguousarray(quad.transpose(0, 2, 1))
    return tuple(jnp.asarray(x) for x in (row, quad, quad_t))


def dot(a, b):
    return jnp.dot(a, b, preferred_element_type=F32)


def tent(offsets):
    return jnp.maximum(0.0, 1.0 - jnp.abs(offsets))


def two_taps(index, shift):
    whole = jnp.floor(shift)
    frac = shift - whole
    tap = whole.astype(jnp.int32)
    tap, next_tap = tap.astype(index.dtype), (tap + 1).astype(index.dtype)
    low = jnp.full(index.shape, 1.0 - frac, F32).astype(BF16)
    high = jnp.full(index.shape, frac, F32).astype(BF16)
    zero = jnp.zeros(index.shape, BF16)
    return jnp.where(index == tap, low, jnp.where(index == next_tap, high, zero))


def project_kernel(
    rows, window, slot_hbm, orient_hbm, lo_hbm, hi_hbm, map_ref, out_ref,
    slabs, diff_y, right, acc, sems, slot_ref, orient_ref, lo_ref, hi_ref, param_sems, *shifted,
):
    slots, depth, box = map_ref.shape[0], map_ref.shape[1], map_ref.shape[2]
    half = box // 2
    me = lax.axis_index("mic")
    orient = (me % 2) * 2 + (me // 2) % 2
    first = (me // 4) * rows
    base = jnp.clip(first - 32, 0, box - window)
    base = pl.multiple_of(base // 16 * 16, 16)

    def fetch(i):
        return pltpu.make_async_copy(map_ref.at[i, :, pl.ds(base, window), :], slabs.at[i], sems.at[i])

    params = [
        pltpu.make_async_copy(src, dst, param_sems.at[n])
        for n, (src, dst) in enumerate(((slot_hbm, slot_ref), (orient_hbm, orient_ref), (lo_hbm, lo_ref), (hi_hbm, hi_ref)))
    ]
    for copy in params:
        copy.start()
    for i in range(slots):
        fetch(i).start()

    d = lax.broadcasted_iota(jnp.int32, (box, box), 0)
    c = lax.broadcasted_iota(jnp.int32, (box, box), 1)
    diff_y[...] = (d - c).astype(diff_y.dtype)
    acc[...] = jnp.zeros_like(acc)
    right[...] = jnp.zeros_like(right)
    for ref in shifted:
        ref[...] = jnp.zeros_like(ref)
    bands = ((slice(0, half + 32), slice(0, half)), (slice(half - 32, box), slice(half, box)))
    place = pl.ds(pl.multiple_of(base - first + 64, 16), window)

    for copy in params:
        copy.wait()
    step = jnp.full((8, 128), orient_ref[orient], jnp.int32).astype(F32)
    radius = MAX_SLOPE * jnp.sqrt((step + 0.5) / NORI)
    slope_x = jnp.max(radius * jnp.cos(GOLDEN_ANGLE * step))
    slope_y = jnp.max(radius * jnp.sin(GOLDEN_ANGLE * step))
    low, high = lo_ref[orient], hi_ref[orient]

    for i in range(slots):
        fetch(i).wait()
        slab = slot_ref[i]

        @pl.when((slab >= low) & (slab < high))
        def _():
            depths = [(slab * depth + j).astype(F32) - (SLABS * SLAB_Z - 1) / 2.0 for j in range(depth)]

            def across(j):
                for ds, cs in bands:
                    right[j, ds, cs] = two_taps(diff_y[ds, cs], slope_y * depths[j])
                moved = dot(slabs[i, j], right[j])
                shifted[2 * j][place, :] = moved[:, :half]
                shifted[2 * j + 1][place, :] = moved[:, half:]

            def down(j, total):
                shift = slope_x * depths[j]
                whole = jnp.floor(shift)
                start = whole.astype(jnp.int32) + 64
                near = jnp.full((1, half), 1.0 - (shift - whole), F32).astype(BF16).astype(F32)
                far = jnp.full((1, half), shift - whole, F32).astype(BF16).astype(F32)
                return [
                    total[n] + near * shifted[2 * j + n][pl.ds(start, rows), :] + far * shifted[2 * j + n][pl.ds(start + 1, rows), :]
                    for n in range(2)
                ]

            total = [acc[0], acc[1]]
            across(0)
            for j in range(depth):
                if j + 1 < depth:
                    across(j + 1)
                total = down(j, total)
            acc[0], acc[1] = total

    out_ref[:, :half] = acc[0].astype(BF16)
    out_ref[:, half:] = acc[1].astype(BF16)


def project(map_slabs, slot_slab, orient_index, slab_lo, slab_hi, rows):
    slots, depth, box = map_slabs.shape[:3]
    blocks = box // rows
    window = min(box, rows + 32 * min(2, blocks - 1))
    args = [pltpu.with_memory_space_constraint(x, pltpu.HBM) for x in (slot_slab, orient_index, slab_lo, slab_hi, map_slabs)]
    return pl.pallas_call(
        lambda *refs: project_kernel(rows, window, *refs),
        out_shape=jax.ShapeDtypeStruct((rows, box), BF16),
        in_specs=[pl.BlockSpec(memory_space=pltpu.HBM)] * 5,
        out_specs=pl.BlockSpec(memory_space=pltpu.VMEM),
        scratch_shapes=[
            pltpu.VMEM((slots, depth, window, box), BF16),
            pltpu.VMEM((box, box), TAP),
            pltpu.VMEM((depth, box, box), BF16),
            pltpu.VMEM((2, rows, box // 2), F32),
            pltpu.SemaphoreType.DMA((slots,)),
            pltpu.SMEM(slot_slab.shape, jnp.int32),
            pltpu.SMEM(orient_index.shape, jnp.int32),
            pltpu.SMEM(orient_index.shape, jnp.int32),
            pltpu.SMEM(orient_index.shape, jnp.int32),
            pltpu.SemaphoreType.DMA((4,)),
        ]
        + [pltpu.VMEM((window + 96, box // 2), F32)] * (2 * depth),
        compiler_params=pltpu.CompilerParams(vmem_limit_bytes=16 << 20),
        name="project",
    )(*args)


def total_kernel(*refs):
    total = refs[0][...].astype(F32)
    for ref in refs[1:-1]:
        total = total + ref[...].astype(F32)
    refs[-1][...] = total.astype(BF16)


def total_of(parts):
    vmem = pl.BlockSpec(memory_space=pltpu.VMEM)
    return pl.pallas_call(
        total_kernel,
        out_shape=jax.ShapeDtypeStruct(parts[0].shape, BF16),
        in_specs=[vmem] * len(parts),
        out_specs=vmem,
        compiler_params=pltpu.CompilerParams(vmem_limit_bytes=2 << 20),
        name="total",
    )(*parts)


def hermitian_kernel(tile_ref, real_ref, imag_ref, picked):
    edge = real_ref.shape[0]
    quarter = edge // 4

    def pick(dim):
        shape = (2 * edge, edge) if dim == 0 else (edge, 2 * edge)
        place = lax.broadcasted_iota(jnp.int32, shape, dim)
        freq = lax.broadcasted_iota(jnp.int32, shape, 1 - dim)
        inner = place & (edge - 1)
        wanted = 4 * (inner & (quarter - 1)) + inner // quarter
        wanted = jnp.where(place < edge, wanted, (edge - wanted) & (edge - 1))
        return freq == wanted

    rows = jnp.where(pick(0), 1.0, 0.0).astype(BF16)
    picked[...] = dot(rows, tile_ref[...]).astype(BF16)
    cols = jnp.where(pick(1), 0.5, 0.0).astype(BF16)
    cols = jnp.concatenate([cols[:, :edge], cols[:, edge:]], axis=0)
    real = jnp.concatenate([picked[:edge, :edge], picked[edge:, :edge]], axis=1)
    real_ref[...] = dot(real, cols)
    imag = jnp.concatenate([picked[:edge, edge:], -picked[edge:, edge:]], axis=1)
    imag_ref[...] = dot(imag, cols)


def hermitian(tile):
    edge = tile.shape[0]
    vmem = pl.BlockSpec(memory_space=pltpu.VMEM)
    return pl.pallas_call(
        hermitian_kernel,
        out_shape=[jax.ShapeDtypeStruct((edge, edge), F32)] * 2,
        in_specs=[vmem],
        out_specs=[vmem] * 2,
        scratch_shapes=[pltpu.VMEM((2 * edge, 2 * edge), BF16)],
        compiler_params=pltpu.CompilerParams(vmem_limit_bytes=16 << 20),
        cost_estimate=pl.CostEstimate(flops=8 * edge**3 * 2, bytes_accessed=12 * edge * edge, transcendentals=0),
        name="hermitian",
    )(tile)


def half_transform(pieces_ref, real_ref, imag_ref, row_ref, quad_ref, quadt_ref, stack, half):
    count, rows, box = pieces_ref.shape
    edge = real_ref.shape[0]
    quarter = edge // 4
    for q in range(count):
        stack[(q // 2) * rows : (q // 2 + 1) * rows, (q % 2) * box : (q % 2 + 1) * box] = pieces_ref[q]
    width = 2 * quarter
    inputs = {}
    rows_of = {}

    def row(gh, part):
        start = part * edge + gh * width
        rows_of[gh, part] = dot(stack[...], row_ref[:, start : start + width])

    def fold(gh):
        rr, ri = rows_of[gh, 0], rows_of[gh, 1]
        r0, r1 = rr[:quarter], rr[quarter:]
        i0, i1 = ri[:quarter], ri[quarter:]
        for r, pair in enumerate(((r0 + r1, i0 + i1), (r0 + i1, i0 - r1), (r0 - r1, i0 - i1), (r0 - i1, i0 + r1))):
            inputs[gh, r] = jnp.concatenate(pair, axis=0).astype(BF16)

    items = [(gh, r) for gh in range(edge // width) for r in range(4)]
    parts = {}

    def spectrum(gh, r):
        return dot(quad_ref[r], inputs[gh, r])

    def back(gh, r, spec):
        cols = slice(gh * width, (gh + 1) * width)
        sr, si = spec[:quarter], spec[quarter:]
        fr = slice(r * quarter, (r + 1) * quarter)
        tr, ti = real_ref[fr, cols], imag_ref[fr, cols]
        product = jnp.concatenate([tr * sr + ti * si, ti * sr - tr * si], axis=0).astype(BF16)
        parts[gh, r] = dot(quadt_ref[r], product)

    def combine(gh):
        part = [parts[gh, r] for r in range(4)]
        ar, ai = part[0][:quarter] + part[2][:quarter], part[0][quarter:] + part[2][quarter:]
        br, bi = part[0][:quarter] - part[2][:quarter], part[0][quarter:] - part[2][quarter:]
        cr, ci = part[1][:quarter] + part[3][:quarter], part[1][quarter:] + part[3][quarter:]
        dr, di = part[1][:quarter] - part[3][:quarter], part[1][quarter:] - part[3][quarter:]
        outs = ((ar + cr, ai + ci), (br - di, bi + dr), (ar - cr, ai - ci), (br + di, bi - dr))
        for k in range(4):
            xs = slice(k * quarter, (k + 1) * quarter)
            hr, hi = outs[k][0].astype(BF16), outs[k][1].astype(BF16)
            for t in range(2):
                lanes = slice(t * quarter, (t + 1) * quarter)
                start = (2 * gh + t) * width
                half[xs, start : start + quarter] = hr[:, lanes]
                half[xs, start + quarter : start + width] = hi[:, lanes]

    specs = {}
    for token in "R0 R1 R2 R3 U0 S0 S1 S2 S3 U1 S4 B0 S5 B1 S6 B2 S7 B3 B4 B5 C0 B6 B7 C1".split():
        act, n = token[0], int(token[1])
        if act == "R":
            row(n // 2, n % 2)
        elif act == "U":
            fold(n)
        elif act == "S":
            specs[n] = spectrum(*items[n])
        elif act == "B":
            back(*items[n], specs.pop(n))
        else:
            combine(n)


def first_kernel(pieces_ref, real_ref, imag_ref, row_ref, quad_ref, quadt_ref, half_ref, stack):
    half_transform(pieces_ref, real_ref, imag_ref, row_ref, quad_ref, quadt_ref, stack, half_ref)


def first_pair(pieces, th_real, th_imag, row, quad, quad_t):
    box, edge = pieces.shape[2], th_real.shape[0]
    vmem = pl.BlockSpec(memory_space=pltpu.VMEM)
    return pl.pallas_call(
        first_kernel,
        out_shape=jax.ShapeDtypeStruct((edge, 2 * edge), BF16),
        in_specs=[vmem] * 6,
        out_specs=vmem,
        scratch_shapes=[pltpu.VMEM((box, 2 * box), BF16)],
        compiler_params=pltpu.CompilerParams(vmem_limit_bytes=12 << 20),
        cost_estimate=pl.CostEstimate(flops=6 * edge**3, bytes_accessed=12 * edge * edge, transcendentals=0),
        name="first_pair",
    )(pieces, th_real, th_imag, row, quad, quad_t)


def columns_of(half, quad_ref, quarter):
    width = 2 * quarter
    return [dot(half[:, s * width : (s + 1) * width], quad_ref[s]) for s in range(4)]


def scores_of(f, quarter):
    re = [x[:, :quarter] for x in f]
    im = [x[:, quarter:] for x in f]
    ar, ai, br, bi = re[0] + re[2], im[0] + im[2], re[0] - re[2], im[0] - im[2]
    cr, ci, dr, di = re[1] + re[3], im[1] + im[3], re[1] - re[3], im[1] - im[3]
    return ((ar + cr, ai + ci), (br - di, bi + dr), (ar - cr, ai - ci), (br + di, bi - dr))


def second_kernel(
    block, pieces_ref, half_ref, real_ref, imag_ref, row_ref, quad_ref, quadt_ref, max_ref, sum_ref, sq_ref,
    best_ref, total_ref, square_ref, stack, other, best_out, total_out, square_out, sems,
):
    edge = max_ref.shape[2]
    quarter = edge // 4
    half_transform(pieces_ref, real_ref, imag_ref, row_ref, quad_ref, quadt_ref, stack, other)
    copies = []
    steps = edge // block

    def columns(step):
        xs = slice(step * block, (step + 1) * block)
        return columns_of(half_ref[xs, :], quad_ref, quarter), columns_of(other[xs, :], quad_ref, quarter)

    ready = columns(0)
    for step in range(steps):
        xs = slice(step * block, (step + 1) * block)
        one, two = (scores_of(x, quarter) for x in ready)
        if step + 1 < steps:
            ready = columns(step + 1)
        for k in range(4):
            ys = slice(k * quarter, (k + 1) * quarter)
            best, total, square = max_ref[0, xs, ys], sum_ref[0, xs, ys], sq_ref[0, xs, ys]
            for score in (*one[k], *two[k]):
                best = jnp.maximum(best, score)
                total = total + score
                square = square + score * score
            best_out[xs, ys] = best
            total_out[xs, ys] = total
            square_out[xs, ys] = square
        for n, (src, dst) in enumerate(((best_out, best_ref), (total_out, total_ref), (square_out, square_ref))):
            copy = pltpu.make_async_copy(src.at[xs, :], dst.at[0, xs, :], sems.at[step, n])
            copy.start()
            copies.append(copy)
    for copy in copies:
        copy.wait()


def second_pair(pieces, half, th_real, th_imag, row, quad, quad_t, prev_max, prev_sum, prev_sumsq):
    box, edge = pieces.shape[2], th_real.shape[0]
    block = edge // 4
    vmem = pl.BlockSpec(memory_space=pltpu.VMEM)
    return pl.pallas_call(
        lambda *refs: second_kernel(block, *refs),
        out_shape=[jax.ShapeDtypeStruct(prev_max.shape, F32)] * 3,
        in_specs=[vmem] * 10,
        out_specs=[pl.BlockSpec(memory_space=pltpu.HBM)] * 3,
        scratch_shapes=[
            pltpu.VMEM((box, 2 * box), BF16),
            pltpu.VMEM((edge, 2 * edge), BF16),
            pltpu.VMEM((edge, edge), F32),
            pltpu.VMEM((edge, edge), F32),
            pltpu.VMEM((edge, edge), F32),
            pltpu.SemaphoreType.DMA((edge // block, 3)),
        ],
        compiler_params=pltpu.CompilerParams(vmem_limit_bytes=16 << 20),
        cost_estimate=pl.CostEstimate(flops=10 * edge**3, bytes_accessed=40 * edge * edge, transcendentals=0),
        name="second_pair",
    )(pieces, half, th_real, th_imag, row, quad, quad_t, prev_max, prev_sum, prev_sumsq)


def swap(value, axis, offset):
    return lax.ppermute(value, axis, [(i, i ^ offset) for i in range(lax.axis_size(axis))])


def swaps(value, axis, low_bit, count):
    order = sorted(range(1, count), key=lambda k: (k & (k - 1) == 0 and k > 1, k))
    return {k: swap(value, axis, k << low_bit) for k in order}


def assemble_kernel(low_bit, bits, *refs):
    mine = (lax.axis_index("mic") >> low_bit) & ((1 << bits) - 1)
    for k, ref in enumerate(refs[:-1]):
        refs[-1][mine ^ k] = ref[...]


def gather_group(value, low_bit, bits):
    got = swaps(value, "mic", low_bit, 1 << bits)
    vmem = pl.BlockSpec(memory_space=pltpu.VMEM)
    out = pl.pallas_call(
        lambda *refs: assemble_kernel(low_bit, bits, *refs),
        out_shape=jax.ShapeDtypeStruct((1 << bits,) + value.shape, value.dtype),
        in_specs=[vmem] * (1 << bits),
        out_specs=vmem,
        compiler_params=pltpu.CompilerParams(vmem_limit_bytes=4 << 20),
        name="assemble",
    )(value, *(got[k] for k in range(1, 1 << bits)))
    return out.reshape((-1,) + value.shape[1:])


def body(map_slabs, slot_slab, orient_index, slab_lo, slab_hi, tile_spectrum, prev_max, prev_sum, prev_sumsq):
    box, edge = map_slabs.shape[2], tile_spectrum.shape[1]
    devices = lax.axis_size("mic")
    bits = devices.bit_length() - 1
    rows = box * 4 // devices
    row, quad, quad_t = constants(box, edge)

    part = project(map_slabs, slot_slab, orient_index, slab_lo, slab_hi, rows)
    got = list(swaps(part, "proj", 0, lax.axis_size("proj")).values())
    tile, _ = lax.optimization_barrier((tile_spectrum[0], part))
    th_real, th_imag = hermitian(tile)
    got, th_real, th_imag = lax.optimization_barrier((got, th_real, th_imag))
    pieces = total_of([part] + got)[None]
    for low in range(1, bits, 2):
        pieces = gather_group(pieces, low, min(2, bits - low))
    others = swap(pieces, "mic", 1)
    half = first_pair(pieces, th_real, th_imag, row, quad, quad_t)
    return tuple(second_pair(others, half, th_real, th_imag, row, quad, quad_t, prev_max, prev_sum, prev_sumsq))


def solution(mesh):
    tiles = P(("mic", "proj"), None, None)
    in_specs = (P("proj", None, None, None), P("proj"), P(), P(), P(), tiles, tiles, tiles, tiles)
    return jax.shard_map(body, mesh=mesh, in_specs=in_specs, out_specs=(tiles,) * 3, check_vma=False)
```
